32 devices in a mesh: dp: 8 (over z, x), mp: 4 (over y, core).
Axes of the slice: x: 2, y: 2, z: 4, core: 2. Of those that a mesh axis runs over, the one named last changes fastest.
Arguments:
- observations: bfloat16 [26624, 2048], P('dp', 'mp'), may hold values from -140 to 140
- layer_weights: bfloat16 [2, 2048, 2048], P(None, 'dp', 'mp'), may hold values from -0.1875 to 0.1875
- head_weights: bfloat16 [2048, 18], P('mp'), may hold values from -0.1875 to 0.1875
- rewards: float32 [416, 64], P('dp'), may hold values from -6 to 6
- actions: int32 [416, 64], P('dp'), may hold values from 0 to 17
- done_flags: int32 [416, 64], P('dp'), may hold values 0 or 1
- behaviour: float32 [416, 64], P('dp'), may hold values from 0.05 to 1
Outputs:
- targets: float32 [416, 64], P('dp')
The draws below stay inside these ranges and needn't reach their ends.
All inputs are finite; a program needn't handle non-finite values. No bound on the sum of `done_flags` on one device may be relied on, other than what follows from the above.
Results may differ from the reference program's by a relative error of at most 0.0056.
Values may be sent and summed in bfloat16 or wider, within the bound.
No kernel may reach another device: no remote copies, remote signals or barrier semaphores. Data moves between devices by JAX's collectives and lax.ppermute only.
A program may use at most 128 MiB of HBM per device.

```python
import math
import jax
import jax.numpy as jnp
from jax import lax

W = 2048
A = 18
LAYERS = 2
LEN = 64
SEQS = 416
ROWS = 26624


def draw_observations(key, part):
    first, second = jax.random.split(jax.random.fold_in(key, 11), 2)
    scales = jnp.exp(jax.random.uniform(second, (ROWS, 1), jnp.float32) * jnp.log(10.0))
    values = jnp.clip(jax.random.normal(first, (ROWS, W), jnp.float32), -4.0, 4.0) * scales
    return values.astype(jnp.bfloat16)


def touch_ends(result, own_key, smallest, high):
    longest = result.shape.index(max(result.shape))
    spots = []
    for shift in (0, 1):
        where = [jax.random.randint(jax.random.fold_in(own_key, axis), (), 0, length) for axis, length in enumerate(result.shape)]
        where[longest] = (where[longest] + shift) % result.shape[longest]
        spots.append(tuple(where))
    return result.at[spots[0]].set(smallest).at[spots[1]].set(high)


def levels(own_key, shape, pieces, smallest, high):
    gain = 1.0
    for position, parts in pieces:
        heights = jax.random.uniform(jax.random.fold_in(jax.random.fold_in(own_key, 6), position), (parts,), jnp.float32, smallest / len(pieces), high / len(pieces))
        gain = gain * jnp.repeat(jnp.exp(heights), shape[position] // parts).reshape((-1,) + (1,) * (len(shape) - 1 - position))
    return gain


def noise(stream_key, dims, scale, bound, cuts=(), kind=jnp.bfloat16):
    gain = levels(stream_key, dims, cuts, -0.22, 0.18) if cuts else 1.0
    result = jax.random.normal(stream_key, dims, jnp.float32) * scale * gain
    return jnp.minimum(jnp.maximum(result, -bound), bound).astype(kind)


def setup_inputs(seed: int = 0) -> dict:
    streams_of = jax.random.split(jax.random.key(seed), 8)
    observations = draw_observations(jax.random.fold_in(streams_of[7], 71), 0)
    layer_weights = noise(streams_of[1], (LAYERS, W, W), (W // 2) ** -0.5, 0.1875, ((1, 8), (2, 4)))
    head_weights = noise(streams_of[2], (W, A), (W // 2) ** -0.5, 0.1875, ((0, 4),))
    rewards = noise(streams_of[3], (SEQS, LEN), 1.0, 6.0, ((0, 8),), jnp.float32)
    actions = touch_ends(jax.random.randint(streams_of[4], (SEQS, LEN), 0, A), jax.random.fold_in(streams_of[4], 1), 0, A - 1).astype(jnp.int32)
    done_flags = touch_ends((jax.random.randint(streams_of[5], (SEQS, LEN), 0, 16) < 1).astype(jnp.int32), jax.random.fold_in(streams_of[5], 1), 0, 1)
    behaviour = jnp.clip(jnp.exp(math.log(1.0) - 2.9957323 * jax.random.uniform(streams_of[6], (SEQS, LEN), jnp.float32) ** levels(streams_of[6], (SEQS, LEN), ((0, 8),), -0.2, 0.2)), 0.05, 1.0)
    return dict(observations=observations, layer_weights=layer_weights, head_weights=head_weights, rewards=rewards, actions=actions, done_flags=done_flags, behaviour=behaviour)


def retrace(qvals, rewards, actions, done_flags, behaviour):
    seqs = rewards.shape[0]
    length = rewards.shape[1]
    qvals = qvals.reshape(seqs, length, A)
    probs = jax.nn.softmax(4.0 * qvals, axis=-1)
    value = jnp.sum(probs * qvals, axis=-1)
    onehot = (actions[:, :, None] == jnp.arange(A, dtype=jnp.int32)[None, None, :]).astype(qvals.dtype)
    taken = jnp.sum(onehot * qvals, axis=-1)
    chosen = jnp.sum(onehot * probs, axis=-1)
    trace = 0.95 * jnp.minimum(1.0, chosen / behaviour)
    keep = 0.99 * (1.0 - done_flags.astype(qvals.dtype))

    def stepper(later, inputs):
        reward_t, keep_t, value_n, trace_n, taken_n = inputs
        now = reward_t + keep_t * (value_n + trace_n * (later - taken_n))
        return now, now

    inputs = (rewards[:, :-1].T, keep[:, :-1].T, value[:, 1:].T, trace[:, 1:].T, taken[:, 1:].T)
    last = taken[:, length - 1]
    final, earlier = lax.scan(stepper, last, inputs, reverse=True)
    return jnp.concatenate([earlier.T, last[:, None]], axis=1)


def reference(observations, layer_weights, head_weights, rewards, actions, done_flags, behaviour):
    hidden = observations
    for layer in range(LAYERS):
        hidden = jax.nn.relu(jnp.dot(hidden, layer_weights[layer], preferred_element_type=jnp.float32)).astype(jnp.bfloat16)
    qvals = jnp.dot(hidden, head_weights, preferred_element_type=jnp.float32)
    return retrace(qvals, rewards, actions, done_flags, behaviour)
```

```python
import functools

import jax
import jax.numpy as jnp
from jax import lax
from jax.experimental import pallas as pl
from jax.experimental.pallas import tpu as pltpu
from jax.sharding import PartitionSpec as P

LANES = 128


def tiles_of(rows, target):
    unit = LANES if rows % LANES == 0 else rows
    units = rows // unit
    count = max(1, -(-units * unit // target))
    sizes = [units // count + (1 if i < units % count else 0) for i in range(count)]
    starts = [sum(sizes[:i]) for i in range(count)]
    return [(s * unit, n * unit) for s, n in zip(starts, sizes) if n]


def layer_kernel(h_blocks, w_blocks, tiles, headed, added, *refs):
    refs = list(refs)
    pos = refs.pop(0)
    hs = [refs.pop(0) for _ in h_blocks]
    ws = [refs.pop(0) for _ in w_blocks]
    head = refs.pop(0) if headed else None
    before = refs.pop(0) if added else None
    out = refs.pop(0)
    hv, wv = refs.pop(0), refs.pop(0)
    ov = None if headed else refs.pop(0)
    hsem, wsem = refs.pop(0), refs.pop(0)
    osem = None if headed else refs.pop(0)

    at = 0
    w_copies = []
    for w, count in zip(ws, w_blocks):
        _, height, width = w.shape
        for j in range(count):
            row, col = pos[2 * at], pos[2 * at + 1]
            copy = pltpu.make_async_copy(
                w.at[j],
                wv.at[pl.ds(pl.multiple_of(row * height, height), height), pl.ds(pl.multiple_of(col * width, width), width)],
                wsem.at[at],
            )
            copy.start()
            w_copies.append(copy)
            at += 1
    h_copies = []
    base = 2 * at
    for t, (start, size) in enumerate(tiles):
        row_copies = []
        at = 0
        for h, count in zip(hs, h_blocks):
            width = h.shape[1] // count
            for j in range(count):
                col = pos[base + at]
                copy = pltpu.make_async_copy(
                    h.at[pl.ds(start, size), pl.ds(j * width, width)],
                    hv.at[pl.ds(start, size), pl.ds(pl.multiple_of(col * width, width), width)],
                    hsem.at[t, at],
                )
                copy.start()
                row_copies.append(copy)
                at += 1
        h_copies.append(row_copies)
    for copy in w_copies:
        copy.wait()
    out_copies = []
    for t, (start, size) in enumerate(tiles):
        for copy in h_copies[t]:
            copy.wait()
        summed = jnp.dot(hv[pl.ds(start, size), :], wv[...], preferred_element_type=jnp.float32)
        hidden = jnp.maximum(summed, 0.0).astype(jnp.bfloat16)
        if headed:
            part = lax.dot_general(head[...], hidden, (((1,), (1,)), ((), ())), preferred_element_type=jnp.float32)
            if added:
                part = part + before[:, pl.ds(start, size)]
            out[:, pl.ds(start, size)] = part
        else:
            ov[pl.ds(start, size), :] = hidden
            copy = pltpu.make_async_copy(ov.at[pl.ds(start, size)], out.at[pl.ds(start, size)], osem.at[t])
            copy.start()
            out_copies.append(copy)
    for copy in out_copies:
        copy.wait()


def layer(pos, hs, h_blocks, ws, depth, width, head=None, before=None):
    rows = hs[0].shape[0]
    w_blocks = tuple(w.shape[0] for w in ws)
    tiles = tiles_of(rows, 416)
    headed, added = head is not None, before is not None
    vmem = pl.BlockSpec(memory_space=pltpu.VMEM)
    anywhere = pl.BlockSpec(memory_space=pl.ANY)
    scratch = [pltpu.VMEM((rows, depth), jnp.bfloat16), pltpu.VMEM((depth, width), jnp.bfloat16)]
    if not headed:
        scratch.append(pltpu.VMEM((rows, width), jnp.bfloat16))
    scratch += [pltpu.SemaphoreType.DMA((len(tiles), sum(h_blocks))), pltpu.SemaphoreType.DMA((sum(w_blocks),))]
    if not headed:
        scratch.append(pltpu.SemaphoreType.DMA((len(tiles),)))
    if headed:
        out_shape = jax.ShapeDtypeStruct((head.shape[0], rows), jnp.float32)
    else:
        out_shape = jax.ShapeDtypeStruct((rows, width), jnp.bfloat16)
    extra = ([head] if headed else []) + ([before] if added else [])
    return pl.pallas_call(
        functools.partial(layer_kernel, h_blocks, w_blocks, tiles, headed, added),
        out_shape=out_shape,
        in_specs=[pl.BlockSpec(memory_space=pltpu.SMEM)] + [anywhere] * (len(hs) + len(ws)) + [vmem] * len(extra),
        out_specs=vmem if headed else anywhere,
        scratch_shapes=scratch,
        compiler_params=pltpu.CompilerParams(vmem_limit_bytes=48 * 1024 * 1024),
        cost_estimate=pl.CostEstimate(
            flops=2 * rows * depth * width, bytes_accessed=2 * (rows * depth + depth * width + rows * width), transcendentals=0
        ),
    )(pos, *hs, *ws, *extra)


def retrace_kernel(length, q0, q1, rewards, actions, done_flags, behaviour, out):
    q = q0[...] + q1[...]
    count, steps = q.shape
    scaled = 4.0 * q
    weights = jnp.exp(scaled - jnp.max(scaled, axis=0, keepdims=True))
    probs = weights / jnp.sum(weights, axis=0, keepdims=True)
    value = jnp.sum(probs * q, axis=0, keepdims=True)
    hit = lax.broadcasted_iota(jnp.int32, (count, steps), 0) == actions[...]
    taken = jnp.sum(jnp.where(hit, q, 0.0), axis=0, keepdims=True)
    chosen = jnp.sum(jnp.where(hit, probs, 0.0), axis=0, keepdims=True)
    trace = 0.95 * jnp.minimum(1.0, chosen / behaviour[...])
    keep = 0.99 * (1.0 - done_flags[...].astype(jnp.float32))

    def later(x, by):
        return pltpu.roll(x, steps - by, axis=1)

    last = lax.broadcasted_iota(jnp.int32, (1, steps), 1) % length == length - 1
    factor = jnp.where(last, 0.0, keep * later(trace, 1))
    offset = jnp.where(last, taken, rewards[...] + keep * later(value - trace * taken, 1))
    by = 1
    while by < length:
        offset = offset + factor * later(offset, by)
        factor = factor * later(factor, by)
        by *= 2
    out[...] = offset


def retrace(q0, q1, rewards, actions, done_flags, behaviour):
    seqs, length = rewards.shape
    flat = [x.reshape(1, seqs * length) for x in (rewards, actions, done_flags, behaviour)]
    out = pl.pallas_call(
        functools.partial(retrace_kernel, length),
        out_shape=jax.ShapeDtypeStruct((1, seqs * length), jnp.float32),
        in_specs=[pl.BlockSpec(memory_space=pltpu.VMEM)] * 6,
        out_specs=pl.BlockSpec(memory_space=pltpu.VMEM),
    )(q0, q1, *flat)
    return out.reshape(seqs, length)


def per_device(dp, mp, observations, layer_weights, head_weights, rewards, actions, done_flags, behaviour):
    across = mp // 2
    lines = dp // 2
    rank, group = lax.axis_index("mp"), lax.axis_index("dp")
    y, core = rank // 2, rank % 2
    z, x = group // 2, group % 2

    def to_core(a):
        return lax.ppermute(a, "mp", [(i, i ^ 1) for i in range(mp)])

    def to_y(a):
        return lax.ppermute(a, "mp", [(i, i ^ 2) for i in range(mp)])

    def to_x(a):
        return lax.ppermute(a, "dp", [(i, i ^ 1) for i in range(dp)])

    def to_z(a):
        return lax.ppermute(a, "dp", [(i, (i + 2) % dp) for i in range(dp)])

    def place(step, x_flip, y_flip):
        return [((z - step) % lines) * 2 + (x ^ x_flip), y ^ y_flip]

    width = layer_weights.shape[2]
    half = width // 2
    rows = observations.shape[0] // 2

    def y_z_x(own):
        ring = [jnp.concatenate([own, to_y(own)], axis=0)]
        for _ in range(lines - 1):
            ring.append(to_z(ring[-1]))
        pieces, places = [], []
        for step, piece in enumerate(ring):
            pieces += [piece, to_x(piece)]
            for x_flip in (0, 1):
                places += place(step, x_flip, 0) + place(step, x_flip, 1)
        return pieces, places

    def z_x_y(own):
        ring = [own]
        for _ in range(lines - 1):
            ring.append(to_z(ring[-1]))
        near = jnp.concatenate(ring, axis=0)
        far = to_x(near)
        pieces, places = [near, far, to_y(near), to_y(far)], []
        for y_flip in (0, 1):
            for x_flip in (0, 1):
                for step in range(lines):
                    places += place(step, x_flip, y_flip)
        return pieces, places

    first, first_places = y_z_x(layer_weights[:1])
    second_a, second_a_places = y_z_x(layer_weights[1:2, :, :half])
    second_b, second_b_places = z_x_y(layer_weights[1:2, :, half:])

    kept = lax.dynamic_slice_in_dim(observations, y * rows, rows)
    sent = lax.dynamic_slice_in_dim(observations, (1 - y) * rows, rows)
    came = to_y(sent)
    h0 = [kept, to_core(kept), came, to_core(came)]
    h0_places = [rank, rank ^ 1, rank ^ 2, rank ^ 3]

    depth = observations.shape[1] * mp
    h1 = layer(jnp.stack(first_places + h0_places), h0, (1, 1, 1, 1), first, depth, across * width)
    hs = [h1, to_core(h1)]
    h_blocks = (across, across)
    h1_places = [2 * i + core for i in range(across)] + [2 * i + 1 - core for i in range(across)]

    head = head_weights.T
    head_other = to_y(head)
    head_low = jnp.where(y == 0, head, head_other)
    head_high = jnp.where(y == 0, head_other, head)
    head_a = jnp.concatenate([head_low[:, :half], head_high[:, :half]], axis=1)
    head_b = jnp.concatenate([head_low[:, half:], head_high[:, half:]], axis=1)

    q_a = layer(jnp.stack(second_a_places + h1_places), hs, h_blocks, second_a, depth, across * half, head_a)
    q = layer(jnp.stack(second_b_places + h1_places), hs, h_blocks, second_b, depth, across * half, head_b, q_a)

    seqs = rewards.shape[0] // 2
    mine = [lax.dynamic_slice_in_dim(a, y * seqs, seqs) for a in (rewards, actions, done_flags, behaviour)]
    own = retrace(q, to_core(q), *mine)
    other = to_y(own)
    return jnp.concatenate([jnp.where(y == 0, own, other), jnp.where(y == 0, other, own)], axis=0)


def solution(mesh):
    in_specs = (
        P("dp", "mp"),
        P(None, "dp", "mp"),
        P("mp", None),
        P("dp", None),
        P("dp", None),
        P("dp", None),
        P("dp", None),
    )
    out_specs = P("dp", None)
    return jax.shard_map(
        functools.partial(per_device, mesh.shape["dp"], mesh.shape["mp"]),
        mesh=mesh,
        in_specs=in_specs,
        out_specs=out_specs,
        check_vma=False,
    )
```

```python
import functools

import jax
import jax.numpy as jnp
from jax import lax
from jax.experimental import pallas as pl
from jax.experimental.pallas import tpu as pltpu
from jax.sharding import PartitionSpec as P

LANES = 128


def tiles_of(rows, target):
    unit = LANES if rows % LANES == 0 else rows
    units = rows // unit
    count = max(1, -(-units * unit // target))
    sizes = [units // count + (1 if i < units % count else 0) for i in range(count)]
    starts = [sum(sizes[:i]) for i in range(count)]
    return [(s * unit, n * unit) for s, n in zip(starts, sizes) if n]


def cut_kernel(at, source, *refs):
    out, sem = refs[-2:]
    rows = source.shape[-2] if source.ndim == 2 else None
    if rows is None:
        copy = pltpu.make_async_copy(source.at[pl.ds(at[0], out.shape[0])], out, sem)
    else:
        copy = pltpu.make_async_copy(source.at[pl.ds(pl.multiple_of(at[0], 16), out.shape[0])], out, sem)
    copy.start()
    copy.wait()


def cut(source, at, size, after=()):
    shape = (size, *source.shape[1:])
    anywhere = pl.BlockSpec(memory_space=pl.ANY)
    return pl.pallas_call(
        cut_kernel,
        out_shape=jax.ShapeDtypeStruct(shape, source.dtype),
        in_specs=[pl.BlockSpec(memory_space=pltpu.SMEM)] + [anywhere] * (1 + len(after)),
        out_specs=pl.BlockSpec(memory_space=pltpu.VMEM),
        scratch_shapes=[pltpu.SemaphoreType.DMA],
        compiler_params=pltpu.CompilerParams(vmem_limit_bytes=16 * 1024 * 1024),
    )(jnp.asarray(at, jnp.int32).reshape(1), source, *after)


def layer_kernel(h_blocks, w_blocks, sizes, headed, waited, *refs):
    refs = list(refs)
    tiles = len(sizes)
    pos = refs.pop(0)
    hs = [[refs.pop(0) for _ in h_blocks] for _ in sizes]
    ws = [refs.pop(0) for _ in w_blocks]
    head = refs.pop(0) if headed else None
    del refs[:waited]
    outs = [refs.pop(0) for _ in range(1 if headed else tiles)]
    hv, wv = refs.pop(0), refs.pop(0)
    ov = None if headed else refs.pop(0)
    hsem, wsem = refs.pop(0), refs.pop(0)
    osem = None if headed else refs.pop(0)

    at = 0
    w_copies = []
    for w, count in zip(ws, w_blocks):
        _, height, width = w.shape
        for j in range(count):
            row, col = pos[2 * at], pos[2 * at + 1]
            copy = pltpu.make_async_copy(
                w.at[j],
                wv.at[pl.ds(pl.multiple_of(row * height, height), height), pl.ds(pl.multiple_of(col * width, width), width)],
                wsem.at[at],
            )
            copy.start()
            w_copies.append(copy)
            at += 1
    h_copies = []
    base = 2 * at
    start = 0
    for t, size in enumerate(sizes):
        row_copies = []
        at = 0
        for h, count in zip(hs[t], h_blocks):
            width = h.shape[1] // count
            for j in range(count):
                col = pos[base + at]
                copy = pltpu.make_async_copy(
                    h.at[:, pl.ds(j * width, width)],
                    hv.at[pl.ds(start, size), pl.ds(pl.multiple_of(col * width, width), width)],
                    hsem.at[t, at],
                )
                copy.start()
                row_copies.append(copy)
                at += 1
        h_copies.append(row_copies)
        start += size
    for copy in w_copies:
        copy.wait()
    out_copies = []
    start = 0
    for t, size in enumerate(sizes):
        for copy in h_copies[t]:
            copy.wait()
        summed = jnp.dot(hv[pl.ds(start, size), :], wv[...], preferred_element_type=jnp.float32)
        hidden = jnp.maximum(summed, 0.0).astype(jnp.bfloat16)
        if headed:
            outs[0][:, pl.ds(start, size)] = lax.dot_general(
                head[...], hidden, (((1,), (1,)), ((), ())), preferred_element_type=jnp.float32
            )
        else:
            ov[pl.ds(start, size), :] = hidden
            copy = pltpu.make_async_copy(ov.at[pl.ds(start, size)], outs[t], osem.at[t])
            copy.start()
            out_copies.append(copy)
        start += size
    for copy in out_copies:
        copy.wait()


def layer(pos, hs, h_blocks, ws, depth, width, head=None, after=()):
    sizes = [tile[0].shape[0] for tile in hs]
    rows = sum(sizes)
    w_blocks = tuple(w.shape[0] for w in ws)
    headed = head is not None
    vmem = pl.BlockSpec(memory_space=pltpu.VMEM)
    anywhere = pl.BlockSpec(memory_space=pl.ANY)
    scratch = [pltpu.VMEM((rows, depth), jnp.bfloat16), pltpu.VMEM((depth, width), jnp.bfloat16)]
    if not headed:
        scratch.append(pltpu.VMEM((rows, width), jnp.bfloat16))
    scratch += [pltpu.SemaphoreType.DMA((len(sizes), sum(h_blocks))), pltpu.SemaphoreType.DMA((sum(w_blocks),))]
    if headed:
        out_shape = jax.ShapeDtypeStruct((head.shape[0], rows), jnp.float32)
    else:
        scratch.append(pltpu.SemaphoreType.DMA((len(sizes),)))
        out_shape = [jax.ShapeDtypeStruct((size, width), jnp.bfloat16) for size in sizes]
    extra = [head] if headed else []
    pieces = [h for tile in hs for h in tile]
    return pl.pallas_call(
        functools.partial(layer_kernel, h_blocks, w_blocks, sizes, headed, len(after)),
        out_shape=out_shape,
        in_specs=[pl.BlockSpec(memory_space=pltpu.SMEM)]
        + [anywhere] * (len(pieces) + len(ws))
        + [vmem] * len(extra)
        + [anywhere] * len(after),
        out_specs=vmem if headed else [anywhere] * len(sizes),
        scratch_shapes=scratch,
        compiler_params=pltpu.CompilerParams(vmem_limit_bytes=32 * 1024 * 1024),
        cost_estimate=pl.CostEstimate(
            flops=2 * rows * depth * width, bytes_accessed=2 * (rows * depth + depth * width + rows * width), transcendentals=0
        ),
    )(pos, *pieces, *ws, *extra, *after)


def retrace_kernel(length, q0, q1, rewards, actions, done_flags, behaviour, out):
    q = q0[...] + q1[...]
    count, steps = q.shape
    scaled = 4.0 * q
    weights = jnp.exp(scaled - jnp.max(scaled, axis=0, keepdims=True))
    probs = weights / jnp.sum(weights, axis=0, keepdims=True)
    value = jnp.sum(probs * q, axis=0, keepdims=True)
    hit = lax.broadcasted_iota(jnp.int32, (count, steps), 0) == actions[...]
    taken = jnp.sum(jnp.where(hit, q, 0.0), axis=0, keepdims=True)
    chosen = jnp.sum(jnp.where(hit, probs, 0.0), axis=0, keepdims=True)
    trace = 0.95 * jnp.minimum(1.0, chosen / behaviour[...])
    keep = 0.99 * (1.0 - done_flags[...].astype(jnp.float32))

    def later(x, by):
        return pltpu.roll(x, steps - by, axis=1)

    last = lax.broadcasted_iota(jnp.int32, (1, steps), 1) % length == length - 1
    factor = jnp.where(last, 0.0, keep * later(trace, 1))
    offset = jnp.where(last, taken, rewards[...] + keep * later(value - trace * taken, 1))
    by = 1
    while by < length:
        offset = offset + factor * later(offset, by)
        factor = factor * later(factor, by)
        by *= 2
    out[...] = offset


def retrace(q0, q1, rewards, actions, done_flags, behaviour, length):
    return pl.pallas_call(
        functools.partial(retrace_kernel, length),
        out_shape=jax.ShapeDtypeStruct(rewards.shape, jnp.float32),
        in_specs=[pl.BlockSpec(memory_space=pltpu.VMEM)] * 6,
        out_specs=pl.BlockSpec(memory_space=pltpu.VMEM),
    )(q0, q1, rewards, actions, done_flags, behaviour)


def per_device(dp, mp, observations, layer_weights, head_weights, rewards, actions, done_flags, behaviour):
    across = mp // 2
    lines = dp // 2
    rank, group = lax.axis_index("mp"), lax.axis_index("dp")
    y, core = rank // 2, rank % 2
    cycle = list(range(0, dp, 2)) + list(range(dp - 1, 0, -2))
    at = jnp.where(group % 2 == 0, group // 2, dp - 1 - group // 2)

    def over(axis, pairs):
        return lambda a: lax.ppermute(a, axis, pairs)

    to_core = over("mp", [(i, i ^ 1) for i in range(mp)])
    to_y = over("mp", [(i, i ^ 2) for i in range(mp)])
    to_next = over("dp", [(cycle[i], cycle[(i + 1) % dp]) for i in range(dp)])
    to_last = over("dp", [(cycle[(i + 1) % dp], cycle[i]) for i in range(dp)])

    def member(steps):
        spot = (at - steps) % dp
        return jnp.where(spot < lines, 2 * spot, 2 * (dp - 1 - spot) + 1)

    def places(steps, flips):
        return [p for step in steps for flip in flips for p in (member(step), y ^ flip)]

    def one_way(send, own, other, hops):
        pairs = send(own)
        came = [pairs]
        if hops > 1:
            pairs = send(jnp.concatenate([pairs, other], axis=0))
            came.append(pairs)
        for _ in range(hops - 2):
            pairs = send(pairs)
            came.append(pairs)
        came.append(send(pairs[1:] if hops > 1 else other))
        return came

    def step_places(sign, hops):
        found = places([sign], (0,))
        for hop in range(2, hops + 1):
            found += places([sign * hop], (0,)) + places([sign * (hop - 1)], (1,))
        return found + places([sign * hops], (1,))

    width = layer_weights.shape[2]
    rows = observations.shape[0] // 2
    depth = observations.shape[1] * mp

    w1 = layer_weights[:1]
    w1_y = to_y(w1)
    w1_next = one_way(to_next, w1, w1_y, lines)
    w1_last = one_way(to_last, w1, w1_y, dp - 1 - lines)
    w2 = cut(layer_weights, 1, 1, [w1_y])
    w2_y = to_y(w2)
    w2_own = cut(layer_weights, 1, 1, [w1_next[0], w1_last[0]])
    w2_next = one_way(to_next, w2_own, w2_y, dp - 1 - lines)
    w2_last = one_way(to_last, w2_own, w2_y, lines)

    tiles = tiles_of(rows, 416)
    came = []
    for i, (start, size) in enumerate(tiles):
        waits = [w1_y] if i == 0 else [w1_next[min(i, lines)], w1_last[min(i, dp - 1 - lines)], w2_y if i == 1 else came[i - 2]]
        came.append(to_y(cut(observations, (1 - y) * rows + start, size, waits)))
    kept = [cut(observations, y * rows + start, size) for start, size in tiles]
    h0 = [[k, to_core(k), c, to_core(c)] for k, c in zip(kept, came)]
    h0_places = [rank, rank ^ 1, rank ^ 2, rank ^ 3]

    seqs = rewards.shape[0] // 2
    flat = [lax.dynamic_slice_in_dim(a, y * seqs, seqs).reshape(1, -1) for a in (rewards, actions, done_flags, behaviour)]
    head = head_weights.T
    head_y = to_y(head)
    heads = jnp.concatenate([jnp.where(y == 0, head, head_y), jnp.where(y == 0, head_y, head)], axis=1)

    first_places = jnp.stack(places([0], (0, 1)) + step_places(1, lines) + step_places(-1, dp - 1 - lines) + h0_places)
    h1 = []
    for part, after in (
        (h0[:2], [w2_next[0], w2_last[1], heads, *flat]),
        (h0[2:], [w2_next[1]]),
    ):
        h1 += layer(
            first_places, part, (1, 1, 1, 1), [w1, w1_y, *w1_next, *w1_last], depth, across * width, after=after
        )
    h1_places = [2 * i + core for i in range(across)] + [2 * i + 1 - core for i in range(across)]
    second_places = places([0], (0, 1)) + step_places(1, dp - 1 - lines) + step_places(-1, lines)
    q = layer(
        jnp.stack(second_places + h1_places),
        [[h, to_core(h)] for h in h1],
        (across, across),
        [w2, w2_y, *w2_next, *w2_last],
        depth,
        across * width,
        heads,
    )
    own = retrace(q, to_core(q), *flat, rewards.shape[1])
    other = to_y(own)
    whole = jnp.concatenate([jnp.where(y == 0, own, other), jnp.where(y == 0, other, own)], axis=1)
    return whole.reshape(rewards.shape)


def solution(mesh):
    in_specs = (
        P("dp", "mp"),
        P(None, "dp", "mp"),
        P("mp", None),
        P("dp", None),
        P("dp", None),
        P("dp", None),
        P("dp", None),
    )
    out_specs = P("dp", None)
    return jax.shard_map(
        functools.partial(per_device, mesh.shape["dp"], mesh.shape["mp"]),
        mesh=mesh,
        in_specs=in_specs,
        out_specs=out_specs,
        check_vma=False,
    )
```

```python
import functools

import jax
import jax.numpy as jnp
from jax import lax
from jax.experimental import pallas as pl
from jax.experimental.pallas import tpu as pltpu
from jax.sharding import PartitionSpec as P

LANES = 128
TILE = 416


def tiles_of(rows, target):
    unit = LANES if rows % LANES == 0 else rows
    units = rows // unit
    count = max(1, -(-units * unit // target))
    sizes = [units // count + (1 if i < units % count else 0) for i in range(count)]
    starts = [sum(sizes[:i]) for i in range(count)]
    return [(s * unit, n * unit) for s, n in zip(starts, sizes) if n]


FREE = pl.CostEstimate(flops=0, bytes_accessed=0, transcendentals=0)


def cut_kernel(count, at, source, *refs):
    outs, sems = refs[-1 - count : -1], refs[-1]
    copies = []
    for i, out in enumerate(outs):
        first = at[i] if source.ndim > 2 else pl.multiple_of(at[i], 16)
        copies.append(pltpu.make_async_copy(source.at[pl.ds(first, out.shape[0])], out, sems.at[i]))
        copies[-1].start()
    for copy in copies:
        copy.wait()


def cut(source, at, sizes):
    return pl.pallas_call(
        functools.partial(cut_kernel, len(sizes)),
        out_shape=[jax.ShapeDtypeStruct((size, *source.shape[1:]), source.dtype) for size in sizes],
        in_specs=[pl.BlockSpec(memory_space=pltpu.SMEM), pl.BlockSpec(memory_space=pl.ANY)],
        out_specs=[pl.BlockSpec(memory_space=pltpu.VMEM)] * len(sizes),
        scratch_shapes=[pltpu.SemaphoreType.DMA((len(sizes),))],
        compiler_params=pltpu.CompilerParams(vmem_limit_bytes=40 * 1024 * 1024),
        cost_estimate=FREE,
    )(jnp.stack([jnp.asarray(a, jnp.int32) for a in at]), source)


def gate_kernel(messages, pieces, *refs):
    outs, sems = refs[-1 - len(messages) : -1], refs[-1]
    copies = []
    for out, message in zip(outs, messages):
        to = 0
        for operand, start, count in message:
            copies.append(
                pltpu.make_async_copy(refs[operand].at[pl.ds(start, count)], out.at[pl.ds(to, count)], sems.at[len(copies)])
            )
            copies[-1].start()
            to += count
    for copy in copies:
        copy.wait()


def gate(messages, after=()):
    arrays, plan, shapes = [], [], []
    for message in messages:
        plan.append([])
        for array, start, count in message:
            if not any(array is other for other in arrays):
                arrays.append(array)
            plan[-1].append(([array is other for other in arrays].index(True), start, count))
        first = message[0][0]
        shapes.append(jax.ShapeDtypeStruct((sum(n for _, _, n in message), *first.shape[1:]), first.dtype))
    pieces = sum(len(message) for message in messages)
    held = sum(shape.size * shape.dtype.itemsize for shape in shapes)
    return pl.pallas_call(
        functools.partial(gate_kernel, plan, pieces),
        out_shape=shapes,
        in_specs=[pl.BlockSpec(memory_space=pl.ANY)] * (len(arrays) + len(after)),
        out_specs=[pl.BlockSpec(memory_space=pltpu.VMEM)] * len(shapes),
        scratch_shapes=[pltpu.SemaphoreType.DMA((pieces,))],
        compiler_params=pltpu.CompilerParams(vmem_limit_bytes=held + 1024 * 1024),
        cost_estimate=FREE,
    )(*arrays, *after)


def layer_kernel(kinds, blocks, tiles, width, headed, added, waited, *refs):
    refs = list(refs)
    pos = refs.pop(0)
    hs = [[refs.pop(0) for _ in range(kind)] for kind in kinds]
    ws = [refs.pop(0) for _ in blocks]
    head = refs.pop(0) if headed else None
    before = refs.pop(0) if added else None
    del refs[:waited]
    hv, wv = refs[-6:-4] if not headed else refs[-4:-2]
    count = wv.shape[1] // width
    outs = [refs.pop(0) for _ in range(1 if headed else count)]
    refs = refs[2:]
    ov = None if headed else refs.pop(0)
    hsem, wsem = refs.pop(0), refs.pop(0)
    osem = None if headed else refs.pop(0)

    w_copies = []
    for i, (w, (j, col)) in enumerate(zip(ws, blocks)):
        height = w.shape[1]
        to = wv.at[pl.ds(pl.multiple_of(pos[i] * height, height), height), pl.ds(col * width, width)]
        w_copies.append(pltpu.make_async_copy(w.at[j], to, wsem.at[i]))
    h_copies = []
    for t, (start, size) in enumerate(tiles):
        h_copies.append([])
        for i, h in enumerate(hs):
            wide = h[0].shape[1]
            to = hv.at[pl.ds(start, size), pl.ds(pl.multiple_of(pos[len(blocks) + i] * wide, wide), wide)]
            source = h[t] if len(h) > 1 else h[0].at[pl.ds(start, size)]
            h_copies[-1].append(pltpu.make_async_copy(source, to, hsem.at[t, i]))
    for copy in h_copies[0] + w_copies:
        copy.start()
    for copy in w_copies:
        copy.wait()
    out_copies = []
    for t, (start, size) in enumerate(tiles):
        for copy in h_copies[t]:
            copy.wait()
        if t + 1 < len(tiles):
            for copy in h_copies[t + 1]:
                copy.start()
        summed = jnp.dot(hv[pl.ds(start, size), :], wv[...], preferred_element_type=jnp.float32)
        hidden = jnp.maximum(summed, 0.0).astype(jnp.bfloat16)
        if headed:
            q = lax.dot_general(head[...], hidden, (((1,), (1,)), ((), ())), preferred_element_type=jnp.float32)
            if added:
                q = q + before[:, pl.ds(start, size)]
            outs[0][:, pl.ds(start, size)] = q
        else:
            ov[pl.ds(start, size), :] = hidden
            for col, out in enumerate(outs):
                source = ov.at[pl.ds(start, size), pl.ds(col * width, width)]
                out_copies.append(pltpu.make_async_copy(source, out.at[pl.ds(start, size)], osem.at[t, col]))
                out_copies[-1].start()
    for copy in out_copies:
        copy.wait()


def layer(pos, hs, ws, head=None, before=None, after=()):
    rows = hs[0][0].shape[0]
    tiles = tiles_of(rows, TILE)
    blocks = [(j, col) for _, j, col in ws]
    ws = [w for w, _, _ in ws]
    count = 1 + max(col for _, col in blocks)
    width = ws[0].shape[2]
    depth = ws[0].shape[1] * len(ws) // count
    headed, added = head is not None, before is not None
    vmem = pl.BlockSpec(memory_space=pltpu.VMEM)
    anywhere = pl.BlockSpec(memory_space=pl.ANY)
    scratch = [pltpu.VMEM((rows, depth), jnp.bfloat16), pltpu.VMEM((depth, width * count), jnp.bfloat16)]
    if not headed:
        scratch.append(pltpu.VMEM((rows, width * count), jnp.bfloat16))
    scratch += [pltpu.SemaphoreType.DMA((len(tiles), len(hs))), pltpu.SemaphoreType.DMA((len(ws),))]
    if headed:
        out_shape = jax.ShapeDtypeStruct((head.shape[0], rows), jnp.float32)
    else:
        scratch.append(pltpu.SemaphoreType.DMA((len(tiles), count)))
        out_shape = [jax.ShapeDtypeStruct((rows, width), jnp.bfloat16)] * count
    extra = ([head] if headed else []) + ([before] if added else [])
    return pl.pallas_call(
        functools.partial(layer_kernel, [len(h) for h in hs], blocks, tiles, width, headed, added, len(after)),
        out_shape=out_shape,
        in_specs=[pl.BlockSpec(memory_space=pltpu.SMEM)]
        + [anywhere] * (sum(len(h) for h in hs) + len(ws))
        + [vmem] * len(extra)
        + [anywhere] * len(after),
        out_specs=vmem if headed else [anywhere] * count,
        scratch_shapes=scratch,
        compiler_params=pltpu.CompilerParams(vmem_limit_bytes=24 * 1024 * 1024),
        cost_estimate=pl.CostEstimate(flops=2 * rows * depth * width * count, bytes_accessed=0, transcendentals=0),
    )(pos, *[a for h in hs for a in h], *ws, *extra, *after)


def retrace_kernel(length, q0, q1, rewards, actions, done_flags, behaviour, out):
    q = q0[...] + q1[...]
    count, steps = q.shape
    scaled = 4.0 * q
    weights = jnp.exp(scaled - jnp.max(scaled, axis=0, keepdims=True))
    probs = weights / jnp.sum(weights, axis=0, keepdims=True)
    value = jnp.sum(probs * q, axis=0, keepdims=True)
    hit = lax.broadcasted_iota(jnp.int32, (count, steps), 0) == actions[...]
    taken = jnp.sum(jnp.where(hit, q, 0.0), axis=0, keepdims=True)
    chosen = jnp.sum(jnp.where(hit, probs, 0.0), axis=0, keepdims=True)
    trace = 0.95 * jnp.minimum(1.0, chosen / behaviour[...])
    keep = 0.99 * (1.0 - done_flags[...].astype(jnp.float32))

    def later(x, by):
        return pltpu.roll(x, steps - by, axis=1)

    last = lax.broadcasted_iota(jnp.int32, (1, steps), 1) % length == length - 1
    factor = jnp.where(last, 0.0, keep * later(trace, 1))
    offset = jnp.where(last, taken, rewards[...] + keep * later(value - trace * taken, 1))
    by = 1
    while by < length:
        offset = offset + factor * later(offset, by)
        factor = factor * later(factor, by)
        by *= 2
    out[...] = offset


def retrace(q0, q1, rewards, actions, done_flags, behaviour, length):
    return pl.pallas_call(
        functools.partial(retrace_kernel, length),
        out_shape=jax.ShapeDtypeStruct(rewards.shape, jnp.float32),
        in_specs=[pl.BlockSpec(memory_space=pltpu.VMEM)] * 6,
        out_specs=pl.BlockSpec(memory_space=pltpu.VMEM),
    )(q0, q1, rewards, actions, done_flags, behaviour)


def per_device(dp, mp, observations, layer_weights, head_weights, rewards, actions, done_flags, behaviour):
    lines = dp // 2
    rank, group = lax.axis_index("mp"), lax.axis_index("dp")
    y = rank // 2
    cycle = list(range(0, dp, 2)) + list(range(dp - 1, 0, -2))
    at = jnp.where(group % 2 == 0, group // 2, dp - 1 - group // 2)

    def over(axis, pairs):
        return lambda a: lax.ppermute(a, axis, pairs)

    to_core = over("mp", [(i, i ^ 1) for i in range(mp)])
    to_y = over("mp", [(i, i ^ 2) for i in range(mp)])
    to_next = over("dp", [(cycle[i], cycle[(i + 1) % dp]) for i in range(dp)])
    to_last = over("dp", [(cycle[(i + 1) % dp], cycle[i]) for i in range(dp)])

    def came_from(step):
        spot = (at - step) % dp
        return jnp.where(spot < lines, 2 * spot, 2 * (dp - 1 - spot) + 1)

    rows = observations.shape[0] // 2
    seqs = rewards.shape[0] // 2
    flat = [lax.dynamic_slice_in_dim(a, y * seqs, seqs).reshape(1, -1) for a in (rewards, actions, done_flags, behaviour)]
    head = head_weights.T
    head_y = to_y(head)

    short, long = dp - 1 - lines, lines
    order = [rank, rank ^ 1, rank ^ 2, rank ^ 3]

    def run(columns, hs, **rest):
        ws, steps = [], []
        for col, (local, chains) in enumerate(columns):
            ws += [(a, j, col) for a, j in ((local, 0), *chains[0], *chains[1])]
            steps += [0, *range(1, len(chains[0]) + 1), *range(-1, -len(chains[1]) - 1, -1)]
        return layer(jnp.stack([came_from(step) for step in steps] + order), hs, ws, **rest)

    kept, sent = cut(observations, [y * rows, (1 - y) * rows], [rows, rows])
    w1, w2 = cut(layer_weights, [0, 1], [1, 1])
    w1_y = to_y(w1)
    kept_c = to_core(kept)
    turns = (long, short)
    ways = ([to_next(w1)], [to_last(w1)])
    sizes = [size for _, size in tiles_of(rows, TILE)]
    parts, start, came, came_c = list(sizes), 0, [], []
    now = [*(way[0] for way in ways), w1_y, head_y]
    for i in range(1, dp):
        if i == 1:
            (w2_gated,) = gate([[(w2, 0, 1)]], now)
            w2_y = to_y(w2_gated)
        build = []
        for way, turn in zip(ways, turns):
            last = way[-1]
            if i == 1:
                build.append([(last, 0, 1), (w1_y, 0, 1)])
            elif i == turn:
                build.append([(last, 1, 1), (w2, 0, 1)])
            elif i == turn + 1:
                build.append([(last, 1, 1), (w2_y, 0, 1)])
            elif i == dp - 1:
                build.append([(last, 1, 1)])
            else:
                build.append(None)
        built = iter(gate([m for m in build if m], now)) if any(build) else None
        messages = [next(built) if m else way[-1] for m, way in zip(build, ways)]
        if parts:
            size = parts.pop(0)
            (part,) = gate([[(sent, start, size)]], [*now, *messages, *(came[-1:] or [w2_y, *flat])])
            start += size
        for send, way, message in zip((to_next, to_last), ways, messages):
            way.append(send(message))
        if start and len(came) < len(sizes):
            came.append(to_y(part))
            came_c.append(to_core(came[-1]))
        now = [way[-1] for way in ways]
        if i == long + 1:
            first = [[], []]
            for way, turn in zip(ways, turns):
                first[0].append([(way[h - 1], 0) for h in range(1, turn + 1)])
                first[1].append([(way[h], min(1, way[h].shape[0] - 1) if h < turn else 0) for h in range(1, turn + 1)])
            h1 = run([(w1, first[0]), (w1_y, first[1])], [[kept], [kept_c], came, came_c], after=flat)
            now = [*now, h1[0]]
            mine, theirs = gate([[(h1[0], 0, rows)], [(h1[1], 0, rows)]], now)
            h1 = [[mine], [to_core(mine)], [theirs], [to_core(theirs)]]
    second = [[], []]
    for way, turn in zip(ways, turns):
        second[0].append([(way[h], 1 if h == turn else 0) for h in range(turn, dp - 1)])
        second[1].append([(way[h + 1], 1 if h + 1 < dp - 1 else 0) for h in range(turn, dp - 1)])
    q = run([(w2, second[0])], h1, head=head, after=[ways[0][-2], ways[1][-2]])
    q = run([(w2_y, second[1])], h1, head=head_y, before=q)
    own = retrace(q, to_core(q), *flat, rewards.shape[1])
    other = to_y(own)
    whole = jnp.concatenate([jnp.where(y == 0, own, other), jnp.where(y == 0, other, own)], axis=1)
    return whole.reshape(rewards.shape)


def solution(mesh):
    in_specs = (
        P("dp", "mp"),
        P(None, "dp", "mp"),
        P("mp", None),
        P("dp", None),
        P("dp", None),
        P("dp", None),
        P("dp", None),
    )
    out_specs = P("dp", None)
    return jax.shard_map(
        functools.partial(per_device, mesh.shape["dp"], mesh.shape["mp"]),
        mesh=mesh,
        in_specs=in_specs,
        out_specs=out_specs,
        check_vma=False,
    )
```

```python
import functools

import jax
import jax.numpy as jnp
from jax import lax
from jax.experimental import pallas as pl
from jax.experimental.pallas import tpu as pltpu
from jax.sharding import PartitionSpec as P

LANES = 128
TILE = 416


def tiles_of(rows, target):
    unit = LANES if rows % LANES == 0 else rows
    units = rows // unit
    count = max(1, -(-units * unit // target))
    sizes = [units // count + (1 if i < units % count else 0) for i in range(count)]
    starts = [sum(sizes[:i]) for i in range(count)]
    return [(s * unit, n * unit) for s, n in zip(starts, sizes) if n]


FREE = pl.CostEstimate(flops=0, bytes_accessed=0, transcendentals=0)


def cut_kernel(count, at, source, *refs):
    outs, sems = refs[-1 - count : -1], refs[-1]
    copies = []
    for i, out in enumerate(outs):
        first = at[i] if source.ndim > 2 else pl.multiple_of(at[i], 16)
        copies.append(pltpu.make_async_copy(source.at[pl.ds(first, out.shape[0])], out, sems.at[i]))
        copies[-1].start()
    for copy in copies:
        copy.wait()


def cut(source, at, sizes):
    return pl.pallas_call(
        functools.partial(cut_kernel, len(sizes)),
        out_shape=[jax.ShapeDtypeStruct((size, *source.shape[1:]), source.dtype) for size in sizes],
        in_specs=[pl.BlockSpec(memory_space=pltpu.SMEM), pl.BlockSpec(memory_space=pl.ANY)],
        out_specs=[pl.BlockSpec(memory_space=pltpu.VMEM)] * len(sizes),
        scratch_shapes=[pltpu.SemaphoreType.DMA((len(sizes),))],
        compiler_params=pltpu.CompilerParams(vmem_limit_bytes=40 * 1024 * 1024),
        cost_estimate=FREE,
    )(jnp.stack([jnp.asarray(a, jnp.int32) for a in at]), source)


def gate_kernel(messages, pieces, *refs):
    outs, sems = refs[-1 - len(messages) : -1], refs[-1]
    copies = []
    for out, message in zip(outs, messages):
        to = 0
        for operand, start, count in message:
            copies.append(
                pltpu.make_async_copy(refs[operand].at[pl.ds(start, count)], out.at[pl.ds(to, count)], sems.at[len(copies)])
            )
            copies[-1].start()
            to += count
    for copy in copies:
        copy.wait()


def gate(messages, after=()):
    arrays, plan, shapes = [], [], []
    for message in messages:
        plan.append([])
        for array, start, count in message:
            if not any(array is other for other in arrays):
                arrays.append(array)
            plan[-1].append(([array is other for other in arrays].index(True), start, count))
        first = message[0][0]
        shapes.append(jax.ShapeDtypeStruct((sum(n for _, _, n in message), *first.shape[1:]), first.dtype))
    pieces = sum(len(message) for message in messages)
    held = sum(shape.size * shape.dtype.itemsize for shape in shapes)
    return pl.pallas_call(
        functools.partial(gate_kernel, plan, pieces),
        out_shape=shapes,
        in_specs=[pl.BlockSpec(memory_space=pl.ANY)] * (len(arrays) + len(after)),
        out_specs=[pl.BlockSpec(memory_space=pltpu.VMEM)] * len(shapes),
        scratch_shapes=[pltpu.SemaphoreType.DMA((pieces,))],
        compiler_params=pltpu.CompilerParams(vmem_limit_bytes=held + 1024 * 1024),
        cost_estimate=FREE,
    )(*arrays, *after)


def hold_kernel(*refs):
    pass


def hold(arrays, after):
    anywhere = pl.BlockSpec(memory_space=pl.ANY)
    return pl.pallas_call(
        hold_kernel,
        out_shape=[jax.ShapeDtypeStruct(a.shape, a.dtype) for a in arrays],
        in_specs=[anywhere] * (len(arrays) + len(after)),
        out_specs=[anywhere] * len(arrays),
        input_output_aliases={i: i for i in range(len(arrays))},
        compiler_params=pltpu.CompilerParams(vmem_limit_bytes=1024 * 1024),
        cost_estimate=FREE,
    )(*arrays, *after)


def layer_kernel(kinds, blocks, tiles, width, headed, added, waited, *refs):
    refs = list(refs)
    pos = refs.pop(0)
    hs = [[refs.pop(0) for _ in range(kind)] for kind in kinds]
    ws = [refs.pop(0) for _ in blocks]
    head = refs.pop(0) if headed else None
    before = refs.pop(0) if added else None
    del refs[:waited]
    hv, wv = refs[-6:-4] if not headed else refs[-4:-2]
    count = wv.shape[1] // width
    outs = [refs.pop(0) for _ in range(1 if headed else count)]
    refs = refs[2:]
    ov = None if headed else refs.pop(0)
    hsem, wsem = refs.pop(0), refs.pop(0)
    osem = None if headed else refs.pop(0)

    w_copies = []
    for i, (w, (j, col)) in enumerate(zip(ws, blocks)):
        height = w.shape[1]
        to = wv.at[pl.ds(pl.multiple_of(pos[i] * height, height), height), pl.ds(col * width, width)]
        w_copies.append(pltpu.make_async_copy(w.at[j], to, wsem.at[i]))
    h_copies = []
    for t, (start, size) in enumerate(tiles):
        h_copies.append([])
        for i, h in enumerate(hs):
            wide = h[0].shape[1]
            to = hv.at[pl.ds(start, size), pl.ds(pl.multiple_of(pos[len(blocks) + i] * wide, wide), wide)]
            source = h[t] if len(h) > 1 else h[0].at[pl.ds(start, size)]
            h_copies[-1].append(pltpu.make_async_copy(source, to, hsem.at[t, i]))
    for copy in h_copies[0] + w_copies:
        copy.start()
    for copy in w_copies:
        copy.wait()
    out_copies = []
    for t, (start, size) in enumerate(tiles):
        for copy in h_copies[t]:
            copy.wait()
        if t + 1 < len(tiles):
            for copy in h_copies[t + 1]:
                copy.start()
        summed = jnp.dot(hv[pl.ds(start, size), :], wv[...], preferred_element_type=jnp.float32)
        hidden = jnp.maximum(summed, 0.0).astype(jnp.bfloat16)
        if headed:
            q = lax.dot_general(head[...], hidden, (((1,), (1,)), ((), ())), preferred_element_type=jnp.float32)
            if added:
                q = q + before[:, pl.ds(start, size)]
            outs[0][:, pl.ds(start, size)] = q
        else:
            ov[pl.ds(start, size), :] = hidden
            for col, out in enumerate(outs):
                source = ov.at[pl.ds(start, size), pl.ds(col * width, width)]
                out_copies.append(pltpu.make_async_copy(source, out.at[pl.ds(start, size)], osem.at[t, col]))
                out_copies[-1].start()
    for copy in out_copies:
        copy.wait()


def layer(pos, hs, ws, head=None, before=None, after=()):
    rows = hs[0][0].shape[0]
    tiles = tiles_of(rows, TILE)
    blocks = [(j, col) for _, j, col in ws]
    ws = [w for w, _, _ in ws]
    count = 1 + max(col for _, col in blocks)
    width = ws[0].shape[2]
    depth = ws[0].shape[1] * len(ws) // count
    headed, added = head is not None, before is not None
    vmem = pl.BlockSpec(memory_space=pltpu.VMEM)
    anywhere = pl.BlockSpec(memory_space=pl.ANY)
    scratch = [pltpu.VMEM((rows, depth), jnp.bfloat16), pltpu.VMEM((depth, width * count), jnp.bfloat16)]
    if not headed:
        scratch.append(pltpu.VMEM((rows, width * count), jnp.bfloat16))
    scratch += [pltpu.SemaphoreType.DMA((len(tiles), len(hs))), pltpu.SemaphoreType.DMA((len(ws),))]
    if headed:
        out_shape = jax.ShapeDtypeStruct((head.shape[0], rows), jnp.float32)
    else:
        scratch.append(pltpu.SemaphoreType.DMA((len(tiles), count)))
        out_shape = [jax.ShapeDtypeStruct((rows, width), jnp.bfloat16)] * count
    extra = ([head] if headed else []) + ([before] if added else [])
    return pl.pallas_call(
        functools.partial(layer_kernel, [len(h) for h in hs], blocks, tiles, width, headed, added, len(after)),
        out_shape=out_shape,
        in_specs=[pl.BlockSpec(memory_space=pltpu.SMEM)]
        + [anywhere] * (sum(len(h) for h in hs) + len(ws))
        + [vmem] * len(extra)
        + [anywhere] * len(after),
        out_specs=vmem if headed else [anywhere] * count,
        scratch_shapes=scratch,
        compiler_params=pltpu.CompilerParams(vmem_limit_bytes=56 * 1024 * 1024),
        cost_estimate=pl.CostEstimate(flops=2 * rows * depth * width * count, bytes_accessed=0, transcendentals=0),
    )(pos, *[a for h in hs for a in h], *ws, *extra, *after)


def retrace_kernel(length, q0, q1, rewards, actions, done_flags, behaviour, out):
    q = q0[...] + q1[...]
    count, steps = q.shape
    scaled = 4.0 * q
    weights = jnp.exp(scaled - jnp.max(scaled, axis=0, keepdims=True))
    probs = weights / jnp.sum(weights, axis=0, keepdims=True)
    value = jnp.sum(probs * q, axis=0, keepdims=True)
    hit = lax.broadcasted_iota(jnp.int32, (count, steps), 0) == actions[...]
    taken = jnp.sum(jnp.where(hit, q, 0.0), axis=0, keepdims=True)
    chosen = jnp.sum(jnp.where(hit, probs, 0.0), axis=0, keepdims=True)
    trace = 0.95 * jnp.minimum(1.0, chosen / behaviour[...])
    keep = 0.99 * (1.0 - done_flags[...].astype(jnp.float32))

    def later(x, by):
        return pltpu.roll(x, steps - by, axis=1)

    last = lax.broadcasted_iota(jnp.int32, (1, steps), 1) % length == length - 1
    factor = jnp.where(last, 0.0, keep * later(trace, 1))
    offset = jnp.where(last, taken, rewards[...] + keep * later(value - trace * taken, 1))
    by = 1
    while by < length:
        offset = offset + factor * later(offset, by)
        factor = factor * later(factor, by)
        by *= 2
    out[...] = offset


def retrace(q0, q1, rewards, actions, done_flags, behaviour, length):
    return pl.pallas_call(
        functools.partial(retrace_kernel, length),
        out_shape=jax.ShapeDtypeStruct(rewards.shape, jnp.float32),
        in_specs=[pl.BlockSpec(memory_space=pltpu.VMEM)] * 6,
        out_specs=pl.BlockSpec(memory_space=pltpu.VMEM),
    )(q0, q1, rewards, actions, done_flags, behaviour)


def per_device(dp, mp, observations, layer_weights, head_weights, rewards, actions, done_flags, behaviour):
    lines = dp // 2
    rank, group = lax.axis_index("mp"), lax.axis_index("dp")
    y = rank // 2
    cycle = list(range(0, dp, 2)) + list(range(dp - 1, 0, -2))
    at = jnp.where(group % 2 == 0, group // 2, dp - 1 - group // 2)

    def over(axis, pairs):
        return lambda a: lax.ppermute(a, axis, pairs)

    to_core = over("mp", [(i, i ^ 1) for i in range(mp)])
    to_y = over("mp", [(i, i ^ 2) for i in range(mp)])
    to_next = over("dp", [(cycle[i], cycle[(i + 1) % dp]) for i in range(dp)])
    to_last = over("dp", [(cycle[(i + 1) % dp], cycle[i]) for i in range(dp)])

    def came_from(step):
        spot = (at - step) % dp
        return jnp.where(spot < lines, 2 * spot, 2 * (dp - 1 - spot) + 1)

    rows = observations.shape[0] // 2
    seqs = rewards.shape[0] // 2
    flat = [lax.dynamic_slice_in_dim(a, y * seqs, seqs).reshape(1, -1) for a in (rewards, actions, done_flags, behaviour)]
    head = head_weights.T
    head_y = to_y(head)

    short, long = dp - 1 - lines, lines
    order = [rank, rank ^ 1, rank ^ 2, rank ^ 3]

    def run(columns, hs, **rest):
        ws, steps = [], []
        for col, (local, chains) in enumerate(columns):
            ws += [(a, j, col) for a, j in ((local, 0), *chains[0], *chains[1])]
            steps += [0, *range(1, len(chains[0]) + 1), *range(-1, -len(chains[1]) - 1, -1)]
        return layer(jnp.stack([came_from(step) for step in steps] + order), hs, ws, **rest)

    kept, sent = cut(observations, [y * rows, (1 - y) * rows], [rows, rows])
    w1, w2 = cut(layer_weights, [0, 1], [1, 1])
    w1_y = to_y(w1)
    kept_c = to_core(kept)
    turns = (long, short)
    ways = ([to_next(layer_weights)], [to_last(layer_weights)])
    sizes = [size for _, size in tiles_of(rows, TILE)]
    parts, start, came, came_c = list(sizes), 0, [], []
    now = [*(way[0] for way in ways), w1_y, head_y]
    for i in range(1, dp):
        if i == 1:
            (w2_gated,) = gate([[(w2, 0, 1)]], now)
            w2_y = to_y(w2_gated)
        build = []
        for way, turn in zip(ways, turns):
            last = way[-1]
            if i == 1:
                build.append([(last, 0, 1), (w1_y, 0, 1)])
            elif i == turn:
                build.append([(last, 1, 1), (way[0], 1, 1)])
            elif i == turn + 1:
                build.append([(last, 1, 1), (w2_y, 0, 1)])
            elif i == dp - 2:
                build.append([(last, 1, 1)])
            else:
                build.append(None)
        built = iter(gate([m for m in build if m], now)) if any(build) else None
        messages = [next(built) if m else way[-1] for m, way in zip(build, ways)]
        if parts:
            size = parts.pop(0)
            (part,) = gate([[(sent, start, size)]], [*now, *messages, *(came[-1:] or [w2_y, *flat])])
            start += size
        for send, way, message in zip((to_next, to_last), ways, messages):
            way.append(send(message))
        if start and len(came) < len(sizes):
            came.append(to_y(part))
            came_c.append(to_core(came[-1]))
        now = [way[-1] for way in ways]
        if i == long + 1:
            first = [[], []]
            for way, turn in zip(ways, turns):
                first[0].append([(way[h - 1], 0) for h in range(1, turn + 1)])
                first[1].append([(way[h], 1 if h < turn else 0) for h in range(1, turn + 1)])
            h1 = run([(w1, first[0]), (w1_y, first[1])], [[kept], [kept_c], came, came_c], after=flat)
            mine, theirs = hold(h1, now)
            now = [*now, mine]
            h1 = [[mine], [to_core(mine)], [theirs], [to_core(theirs)]]
    second = [[], []]
    for way, turn in zip(ways, turns):
        second[0].append([(way[0], 1), (way[turn], 1)] + [(way[h], 0) for h in range(turn + 1, dp - 2)])
        second[1].append([(way[h], 1) for h in range(turn + 1, dp - 2)] + [(way[-2], 0), (way[-1], 0)])
    q = run([(w2, second[0])], h1, head=head, after=[ways[0][-2], ways[1][-2]])
    q = run([(w2_y, second[1])], h1, head=head_y, before=q)
    own = retrace(q, to_core(q), *flat, rewards.shape[1])
    other = to_y(own)
    whole = jnp.concatenate([jnp.where(y == 0, own, other), jnp.where(y == 0, other, own)], axis=1)
    return whole.reshape(rewards.shape)


def solution(mesh):
    in_specs = (
        P("dp", "mp"),
        P(None, "dp", "mp"),
        P("mp", None),
        P("dp", None),
        P("dp", None),
        P("dp", None),
        P("dp", None),
    )
    out_specs = P("dp", None)
    return jax.shard_map(
        functools.partial(per_device, mesh.shape["dp"], mesh.shape["mp"]),
        mesh=mesh,
        in_specs=in_specs,
        out_specs=out_specs,
        check_vma=False,
    )
```

```python
import functools

import jax
import jax.numpy as jnp
from jax import lax
from jax.experimental import pallas as pl
from jax.experimental.pallas import tpu as pltpu
from jax.sharding import PartitionSpec as P

LANES = 128
TILE = 416


def tiles_of(rows, target):
    unit = LANES if rows % LANES == 0 else rows
    units = rows // unit
    count = max(1, -(-units * unit // target))
    sizes = [units // count + (1 if i < units % count else 0) for i in range(count)]
    starts = [sum(sizes[:i]) for i in range(count)]
    return [(s * unit, n * unit) for s, n in zip(starts, sizes) if n]


FREE = pl.CostEstimate(flops=0, bytes_accessed=0, transcendentals=0)


def cut_kernel(count, at, source, *refs):
    outs, sems = refs[-1 - count : -1], refs[-1]
    copies = []
    for i, out in enumerate(outs):
        first = at[i] if source.ndim > 2 else pl.multiple_of(at[i], 16)
        copies.append(pltpu.make_async_copy(source.at[pl.ds(first, out.shape[0])], out, sems.at[i]))
        copies[-1].start()
    for copy in copies:
        copy.wait()


def cut(source, at, sizes):
    return pl.pallas_call(
        functools.partial(cut_kernel, len(sizes)),
        out_shape=[jax.ShapeDtypeStruct((size, *source.shape[1:]), source.dtype) for size in sizes],
        in_specs=[pl.BlockSpec(memory_space=pltpu.SMEM), pl.BlockSpec(memory_space=pl.ANY)],
        out_specs=[pl.BlockSpec(memory_space=pltpu.VMEM)] * len(sizes),
        scratch_shapes=[pltpu.SemaphoreType.DMA((len(sizes),))],
        compiler_params=pltpu.CompilerParams(vmem_limit_bytes=40 * 1024 * 1024),
        cost_estimate=FREE,
    )(jnp.stack([jnp.asarray(a, jnp.int32) for a in at]), source)


def gate_kernel(messages, pieces, *refs):
    outs, sems = refs[-1 - len(messages) : -1], refs[-1]
    copies = []
    for out, message in zip(outs, messages):
        to = 0
        for operand, start, count in message:
            copies.append(
                pltpu.make_async_copy(refs[operand].at[pl.ds(start, count)], out.at[pl.ds(to, count)], sems.at[len(copies)])
            )
            copies[-1].start()
            to += count
    for copy in copies:
        copy.wait()


def gate(messages, after=()):
    arrays, plan, shapes = [], [], []
    for message in messages:
        plan.append([])
        for array, start, count in message:
            if not any(array is other for other in arrays):
                arrays.append(array)
            plan[-1].append(([array is other for other in arrays].index(True), start, count))
        first = message[0][0]
        shapes.append(jax.ShapeDtypeStruct((sum(n for _, _, n in message), *first.shape[1:]), first.dtype))
    pieces = sum(len(message) for message in messages)
    held = sum(shape.size * shape.dtype.itemsize for shape in shapes)
    return pl.pallas_call(
        functools.partial(gate_kernel, plan, pieces),
        out_shape=shapes,
        in_specs=[pl.BlockSpec(memory_space=pl.ANY)] * (len(arrays) + len(after)),
        out_specs=[pl.BlockSpec(memory_space=pltpu.VMEM)] * len(shapes),
        scratch_shapes=[pltpu.SemaphoreType.DMA((pieces,))],
        compiler_params=pltpu.CompilerParams(vmem_limit_bytes=held + 1024 * 1024),
        cost_estimate=FREE,
    )(*arrays, *after)


def hold_kernel(*refs):
    pass


def hold(arrays, after):
    anywhere = pl.BlockSpec(memory_space=pl.ANY)
    return pl.pallas_call(
        hold_kernel,
        out_shape=[jax.ShapeDtypeStruct(a.shape, a.dtype) for a in arrays],
        in_specs=[anywhere] * (len(arrays) + len(after)),
        out_specs=[anywhere] * len(arrays),
        input_output_aliases={i: i for i in range(len(arrays))},
        compiler_params=pltpu.CompilerParams(vmem_limit_bytes=1024 * 1024),
        cost_estimate=FREE,
    )(*arrays, *after)


def layer_kernel(kinds, blocks, tiles, width, headed, waited, *refs):
    refs = list(refs)
    pos = refs.pop(0)
    hs = [[refs.pop(0) for _ in range(kind)] for kind in kinds]
    ws = [refs.pop(0) for _ in blocks]
    heads = [refs.pop(0) for _ in range(headed)]
    del refs[:waited]
    hv, wv = refs[-6:-4] if not headed else refs[-4:-2]
    count = wv.shape[1] // width
    outs = [refs.pop(0) for _ in range(1 if headed else count)]
    refs = refs[2:]
    ov = None if headed else refs.pop(0)
    hsem, wsem = refs.pop(0), refs.pop(0)
    osem = None if headed else refs.pop(0)

    w_copies = []
    for i, (w, (j, col)) in enumerate(zip(ws, blocks)):
        height = w.shape[1]
        to = wv.at[pl.ds(pl.multiple_of(pos[i] * height, height), height), pl.ds(col * width, width)]
        w_copies.append(pltpu.make_async_copy(w.at[j], to, wsem.at[i]))
    h_copies = []
    for t, (start, size) in enumerate(tiles):
        h_copies.append([])
        for i, h in enumerate(hs):
            wide = h[0].shape[1]
            to = hv.at[pl.ds(start, size), pl.ds(pl.multiple_of(pos[len(blocks) + i] * wide, wide), wide)]
            source = h[t] if len(h) > 1 else h[0].at[pl.ds(start, size)]
            h_copies[-1].append(pltpu.make_async_copy(source, to, hsem.at[t, i]))
    w_columns = [[copy for copy, (_, at) in zip(w_copies, blocks) if at == col] for col in range(count)]
    for copy in h_copies[0] + w_columns[0]:
        copy.start()
    out_copies = []
    for t, (start, size) in enumerate(tiles):
        rows = pl.ds(start, size)
        for copy in h_copies[t]:
            copy.wait()
        total = None
        for col in range(count):
            if t == 0:
                for copy in w_columns[col]:
                    copy.wait()
                for copy in w_columns[col + 1] if col + 1 < count else []:
                    copy.start()
            if col == 0 and t + 1 < len(tiles):
                for copy in h_copies[t + 1]:
                    copy.start()
            units = pl.ds(col * width, width)
            summed = jnp.dot(hv[rows, :], wv[:, units], preferred_element_type=jnp.float32)
            hidden = jnp.maximum(summed, 0.0).astype(jnp.bfloat16)
            if headed:
                q = lax.dot_general(
                    heads[col][...], hidden, (((1,), (1,)), ((), ())), preferred_element_type=jnp.float32
                )
                total = q if total is None else total + q
            else:
                ov[rows, units] = hidden
                out_copies.append(pltpu.make_async_copy(ov.at[rows, units], outs[col].at[rows], osem.at[t, col]))
                out_copies[-1].start()
        if headed:
            outs[0][:, rows] = total
    for copy in out_copies:
        copy.wait()


def layer(pos, hs, ws, heads=(), after=()):
    rows = hs[0][0].shape[0]
    tiles = tiles_of(rows, TILE)
    blocks = [(j, col) for _, j, col in ws]
    ws = [w for w, _, _ in ws]
    count = 1 + max(col for _, col in blocks)
    width = ws[0].shape[2]
    depth = ws[0].shape[1] * len(ws) // count
    headed = len(heads)
    vmem = pl.BlockSpec(memory_space=pltpu.VMEM)
    anywhere = pl.BlockSpec(memory_space=pl.ANY)
    scratch = [pltpu.VMEM((rows, depth), jnp.bfloat16), pltpu.VMEM((depth, width * count), jnp.bfloat16)]
    if not headed:
        scratch.append(pltpu.VMEM((rows, width * count), jnp.bfloat16))
    scratch += [pltpu.SemaphoreType.DMA((len(tiles), len(hs))), pltpu.SemaphoreType.DMA((len(ws),))]
    if headed:
        out_shape = jax.ShapeDtypeStruct((heads[0].shape[0], rows), jnp.float32)
    else:
        scratch.append(pltpu.SemaphoreType.DMA((len(tiles), count)))
        out_shape = [jax.ShapeDtypeStruct((rows, width), jnp.bfloat16)] * count
    return pl.pallas_call(
        functools.partial(layer_kernel, [len(h) for h in hs], blocks, tiles, width, headed, len(after)),
        out_shape=out_shape,
        in_specs=[pl.BlockSpec(memory_space=pltpu.SMEM)]
        + [anywhere] * (sum(len(h) for h in hs) + len(ws))
        + [vmem] * headed
        + [anywhere] * len(after),
        out_specs=vmem if headed else [anywhere] * count,
        scratch_shapes=scratch,
        compiler_params=pltpu.CompilerParams(vmem_limit_bytes=56 * 1024 * 1024),
        cost_estimate=pl.CostEstimate(flops=2 * rows * depth * width * count, bytes_accessed=0, transcendentals=0),
    )(pos, *[a for h in hs for a in h], *ws, *heads, *after)


def retrace_kernel(length, q0, q1, rewards, actions, done_flags, behaviour, out):
    q = q0[...] + q1[...]
    count, steps = q.shape
    scaled = 4.0 * q
    weights = jnp.exp(scaled - jnp.max(scaled, axis=0, keepdims=True))
    probs = weights / jnp.sum(weights, axis=0, keepdims=True)
    value = jnp.sum(probs * q, axis=0, keepdims=True)
    hit = lax.broadcasted_iota(jnp.int32, (count, steps), 0) == actions[...]
    taken = jnp.sum(jnp.where(hit, q, 0.0), axis=0, keepdims=True)
    chosen = jnp.sum(jnp.where(hit, probs, 0.0), axis=0, keepdims=True)
    trace = 0.95 * jnp.minimum(1.0, chosen / behaviour[...])
    keep = 0.99 * (1.0 - done_flags[...].astype(jnp.float32))

    def later(x, by):
        return pltpu.roll(x, steps - by, axis=1)

    last = lax.broadcasted_iota(jnp.int32, (1, steps), 1) % length == length - 1
    factor = jnp.where(last, 0.0, keep * later(trace, 1))
    offset = jnp.where(last, taken, rewards[...] + keep * later(value - trace * taken, 1))
    by = 1
    while by < length:
        offset = offset + factor * later(offset, by)
        factor = factor * later(factor, by)
        by *= 2
    out[...] = offset


def retrace(q0, q1, rewards, actions, done_flags, behaviour, length):
    return pl.pallas_call(
        functools.partial(retrace_kernel, length),
        out_shape=jax.ShapeDtypeStruct(rewards.shape, jnp.float32),
        in_specs=[pl.BlockSpec(memory_space=pltpu.VMEM)] * 6,
        out_specs=pl.BlockSpec(memory_space=pltpu.VMEM),
    )(q0, q1, rewards, actions, done_flags, behaviour)


def per_device(dp, mp, observations, layer_weights, head_weights, rewards, actions, done_flags, behaviour):
    lines = dp // 2
    rank, group = lax.axis_index("mp"), lax.axis_index("dp")
    y = rank // 2
    cycle = list(range(0, dp, 2)) + list(range(dp - 1, 0, -2))
    at = jnp.where(group % 2 == 0, group // 2, dp - 1 - group // 2)

    def over(axis, pairs):
        return lambda a: lax.ppermute(a, axis, pairs)

    to_core = over("mp", [(i, i ^ 1) for i in range(mp)])
    to_y = over("mp", [(i, i ^ 2) for i in range(mp)])
    to_next = over("dp", [(cycle[i], cycle[(i + 1) % dp]) for i in range(dp)])
    to_last = over("dp", [(cycle[(i + 1) % dp], cycle[i]) for i in range(dp)])

    def came_from(step):
        spot = (at - step) % dp
        return jnp.where(spot < lines, 2 * spot, 2 * (dp - 1 - spot) + 1)

    rows = observations.shape[0] // 2
    seqs = rewards.shape[0] // 2
    flat = [lax.dynamic_slice_in_dim(a, y * seqs, seqs).reshape(1, -1) for a in (rewards, actions, done_flags, behaviour)]
    head = head_weights.T
    head_y = to_y(head)

    short, long = dp - 1 - lines, lines
    order = [rank, rank ^ 1, rank ^ 2, rank ^ 3]

    def run(columns, hs, **rest):
        ws, steps = [], []
        for col, (local, chains) in enumerate(columns):
            ws += [(a, j, col) for a, j in ((local, 0), *chains[0], *chains[1])]
            steps += [0, *range(1, len(chains[0]) + 1), *range(-1, -len(chains[1]) - 1, -1)]
        return layer(jnp.stack([came_from(step) for step in steps] + order), hs, ws, **rest)

    kept, sent = cut(observations, [y * rows, (1 - y) * rows], [rows, rows])
    w1, w2 = cut(layer_weights, [0, 1], [1, 1])
    w1_y = to_y(w1)
    kept_c = to_core(kept)
    turns = (long, short)
    ways = ([to_next(layer_weights)], [to_last(layer_weights)])
    sizes = [size for _, size in tiles_of(rows, TILE)]
    over_y = []
    parts, start, came, came_c = list(sizes), 0, [], []
    now = [*(way[0] for way in ways), w1_y, head_y]
    for i in range(1, dp - 1):
        if i == 1:
            (w2_gated,) = gate([[(w2, 0, 1)]], now)
            w2_y = to_y(w2_gated)
        build = []
        for way, turn in zip(ways, turns):
            last = way[-1]
            if i == 1:
                build.append([(last, 0, 1), (w1_y, 0, 1)])
            elif i == turn:
                build.append([(last, 1, 1), (way[0], 1, 1)])
            elif i == turn + 1:
                build.append([(last, 1, 1), (w2_y, 0, 1)])
            elif i == dp - 2:
                build.append([(over_y[0], len(build), 1)])
            else:
                build.append(None)
        if i == dp - 3:
            build.append([(way[-1], 1 if dp - 1 - turn == 3 else 0, 1) for way, turn in zip(ways, turns)])
        built = iter(gate([m for m in build if m], now)) if any(build) else None
        messages = [next(built) if m else way[-1] for m, way in zip(build, ways)]
        if i == dp - 3:
            over_y = [to_y(next(built))]
        if parts:
            size = parts.pop(0)
            (part,) = gate([[(sent, start, size)]], [*now, *messages, *(came[-1:] or [w2_y, *flat])])
            start += size
        for send, way, message in zip((to_next, to_last), ways, messages):
            way.append(send(message))
        if start and len(came) < len(sizes):
            came.append(to_y(part))
            came_c.append(to_core(came[-1]))
        now = [way[-1] for way in ways]
        if i == long + 1:
            first = [[], []]
            for way, turn in zip(ways, turns):
                first[0].append([(way[h - 1], 0) for h in range(1, turn + 1)])
                first[1].append([(way[h], 1 if h < turn else 0) for h in range(1, turn + 1)])
            h1 = run([(w1, first[0]), (w1_y, first[1])], [[kept], [kept_c], came, came_c], after=flat)
            mine, theirs = hold(h1, now + over_y)
            now = [*now, mine]
            h1 = [[mine], [to_core(mine)], [theirs], [to_core(theirs)]]
    second = [[], []]
    for n, (way, turn) in enumerate(zip(ways, turns)):
        second[0].append([(way[0], 1), (way[turn], 1)] + [(way[h], 0) for h in range(turn + 1, dp - 2)])
        second[1].append([(way[h], 1) for h in range(turn + 1, dp - 2)] + [(over_y[0], n), (way[-1], 0)])
    q = run([(w2, second[0]), (w2_y, second[1])], h1, heads=[head, head_y])
    own = retrace(q, to_core(q), *flat, rewards.shape[1])
    other = to_y(own)
    whole = jnp.concatenate([jnp.where(y == 0, own, other), jnp.where(y == 0, other, own)], axis=1)
    return whole.reshape(rewards.shape)


def solution(mesh):
    in_specs = (
        P("dp", "mp"),
        P(None, "dp", "mp"),
        P("mp", None),
        P("dp", None),
        P("dp", None),
        P("dp", None),
        P("dp", None),
    )
    out_specs = P("dp", None)
    return jax.shard_map(
        functools.partial(per_device, mesh.shape["dp"], mesh.shape["mp"]),
        mesh=mesh,
        in_specs=in_specs,
        out_specs=out_specs,
        check_vma=False,
    )
```

```python
import functools

import jax
import jax.numpy as jnp
from jax import lax
from jax.experimental import pallas as pl
from jax.experimental.pallas import tpu as pltpu
from jax.sharding import PartitionSpec as P

LANES = 128
TILE = 416


def tiles_of(rows, target):
    unit = LANES if rows % LANES == 0 else rows
    units = rows // unit
    count = max(1, -(-units * unit // target))
    sizes = [units // count + (1 if i < units % count else 0) for i in range(count)]
    starts = [sum(sizes[:i]) for i in range(count)]
    return [(s * unit, n * unit) for s, n in zip(starts, sizes) if n]


FREE = pl.CostEstimate(flops=0, bytes_accessed=0, transcendentals=0)


def cut_kernel(count, at, source, *refs):
    outs, sems = refs[-1 - count : -1], refs[-1]
    copies = []
    for i, out in enumerate(outs):
        first = at[i] if source.ndim > 2 else pl.multiple_of(at[i], 16)
        copies.append(pltpu.make_async_copy(source.at[pl.ds(first, out.shape[0])], out, sems.at[i]))
        copies[-1].start()
    for copy in copies:
        copy.wait()


def cut(source, at, sizes):
    return pl.pallas_call(
        functools.partial(cut_kernel, len(sizes)),
        out_shape=[jax.ShapeDtypeStruct((size, *source.shape[1:]), source.dtype) for size in sizes],
        in_specs=[pl.BlockSpec(memory_space=pltpu.SMEM), pl.BlockSpec(memory_space=pl.ANY)],
        out_specs=[pl.BlockSpec(memory_space=pltpu.VMEM)] * len(sizes),
        scratch_shapes=[pltpu.SemaphoreType.DMA((len(sizes),))],
        compiler_params=pltpu.CompilerParams(vmem_limit_bytes=40 * 1024 * 1024),
        cost_estimate=FREE,
    )(jnp.stack([jnp.asarray(a, jnp.int32) for a in at]), source)


def gate_kernel(messages, pieces, *refs):
    outs, sems = refs[-1 - len(messages) : -1], refs[-1]
    copies = []
    for out, message in zip(outs, messages):
        to = 0
        for operand, start, count in message:
            copies.append(
                pltpu.make_async_copy(refs[operand].at[pl.ds(start, count)], out.at[pl.ds(to, count)], sems.at[len(copies)])
            )
            copies[-1].start()
            to += count
    for copy in copies:
        copy.wait()


def gate(messages, after=()):
    arrays, plan, shapes = [], [], []
    for message in messages:
        plan.append([])
        for array, start, count in message:
            if not any(array is other for other in arrays):
                arrays.append(array)
            plan[-1].append(([array is other for other in arrays].index(True), start, count))
        first = message[0][0]
        shapes.append(jax.ShapeDtypeStruct((sum(n for _, _, n in message), *first.shape[1:]), first.dtype))
    pieces = sum(len(message) for message in messages)
    held = sum(shape.size * shape.dtype.itemsize for shape in shapes)
    return pl.pallas_call(
        functools.partial(gate_kernel, plan, pieces),
        out_shape=shapes,
        in_specs=[pl.BlockSpec(memory_space=pl.ANY)] * (len(arrays) + len(after)),
        out_specs=[pl.BlockSpec(memory_space=pltpu.VMEM)] * len(shapes),
        scratch_shapes=[pltpu.SemaphoreType.DMA((pieces,))],
        compiler_params=pltpu.CompilerParams(vmem_limit_bytes=held + 1024 * 1024),
        cost_estimate=FREE,
    )(*arrays, *after)


def hold_kernel(*refs):
    pass


def hold(arrays, after):
    anywhere = pl.BlockSpec(memory_space=pl.ANY)
    return pl.pallas_call(
        hold_kernel,
        out_shape=[jax.ShapeDtypeStruct(a.shape, a.dtype) for a in arrays],
        in_specs=[anywhere] * (len(arrays) + len(after)),
        out_specs=[anywhere] * len(arrays),
        input_output_aliases={i: i for i in range(len(arrays))},
        compiler_params=pltpu.CompilerParams(vmem_limit_bytes=1024 * 1024),
        cost_estimate=FREE,
    )(*arrays, *after)


def layer_kernel(kinds, blocks, tiles, width, headed, waited, *refs):
    refs = list(refs)
    pos = refs.pop(0)
    hs = [[refs.pop(0) for _ in range(kind)] for kind in kinds]
    ws = [refs.pop(0) for _ in blocks]
    heads = [refs.pop(0) for _ in range(headed)]
    del refs[:waited]
    hv, wv = refs[-6:-4] if not headed else refs[-4:-2]
    count = wv.shape[1] // width
    outs = [refs.pop(0) for _ in range(1 if headed else count)]
    refs = refs[2:]
    ov = None if headed else refs.pop(0)
    hsem, wsem = refs.pop(0), refs.pop(0)
    osem = None if headed else refs.pop(0)

    w_copies = []
    for i, (w, (j, col)) in enumerate(zip(ws, blocks)):
        height = w.shape[1]
        to = wv.at[pl.ds(pl.multiple_of(pos[i] * height, height), height), pl.ds(col * width, width)]
        w_copies.append(pltpu.make_async_copy(w.at[j], to, wsem.at[i]))
    h_copies = []
    for t, (start, size) in enumerate(tiles):
        h_copies.append([])
        for i, h in enumerate(hs):
            wide = h[0].shape[1]
            to = hv.at[pl.ds(start, size), pl.ds(pl.multiple_of(pos[len(blocks) + i] * wide, wide), wide)]
            source = h[t] if len(h) > 1 else h[0].at[pl.ds(start, size)]
            h_copies[-1].append(pltpu.make_async_copy(source, to, hsem.at[t, i]))
    w_columns = [[copy for copy, (_, at) in zip(w_copies, blocks) if at == col] for col in range(count)]
    for copy in h_copies[0] + w_columns[0]:
        copy.start()
    out_copies = []
    for t, (start, size) in enumerate(tiles):
        rows = pl.ds(start, size)
        for copy in h_copies[t]:
            copy.wait()
        total = None
        for col in range(count):
            if t == 0:
                for copy in w_columns[col]:
                    copy.wait()
                for copy in w_columns[col + 1] if col + 1 < count else []:
                    copy.start()
            if col == 0 and t + 1 < len(tiles):
                for copy in h_copies[t + 1]:
                    copy.start()
            units = pl.ds(col * width, width)
            summed = jnp.dot(hv[rows, :], wv[:, units], preferred_element_type=jnp.float32)
            hidden = jnp.maximum(summed, 0.0).astype(jnp.bfloat16)
            if headed:
                q = lax.dot_general(
                    heads[col][...], hidden, (((1,), (1,)), ((), ())), preferred_element_type=jnp.float32
                )
                total = q if total is None else total + q
            else:
                ov[rows, units] = hidden
                out_copies.append(pltpu.make_async_copy(ov.at[rows, units], outs[col].at[rows], osem.at[t, col]))
                out_copies[-1].start()
        if headed:
            outs[0][:, rows] = total
    for copy in out_copies:
        copy.wait()


def layer(pos, hs, ws, heads=(), after=()):
    rows = hs[0][0].shape[0]
    tiles = tiles_of(rows, TILE)
    blocks = [(j, col) for _, j, col in ws]
    ws = [w for w, _, _ in ws]
    count = 1 + max(col for _, col in blocks)
    width = ws[0].shape[2]
    depth = ws[0].shape[1] * len(ws) // count
    headed = len(heads)
    vmem = pl.BlockSpec(memory_space=pltpu.VMEM)
    anywhere = pl.BlockSpec(memory_space=pl.ANY)
    scratch = [pltpu.VMEM((rows, depth), jnp.bfloat16), pltpu.VMEM((depth, width * count), jnp.bfloat16)]
    if not headed:
        scratch.append(pltpu.VMEM((rows, width * count), jnp.bfloat16))
    scratch += [pltpu.SemaphoreType.DMA((len(tiles), len(hs))), pltpu.SemaphoreType.DMA((len(ws),))]
    if headed:
        out_shape = jax.ShapeDtypeStruct((heads[0].shape[0], rows), jnp.float32)
    else:
        scratch.append(pltpu.SemaphoreType.DMA((len(tiles), count)))
        out_shape = [jax.ShapeDtypeStruct((rows, width), jnp.bfloat16)] * count
    return pl.pallas_call(
        functools.partial(layer_kernel, [len(h) for h in hs], blocks, tiles, width, headed, len(after)),
        out_shape=out_shape,
        in_specs=[pl.BlockSpec(memory_space=pltpu.SMEM)]
        + [anywhere] * (sum(len(h) for h in hs) + len(ws))
        + [vmem] * headed
        + [anywhere] * len(after),
        out_specs=vmem if headed else [anywhere] * count,
        scratch_shapes=scratch,
        compiler_params=pltpu.CompilerParams(vmem_limit_bytes=52 * 1024 * 1024),
        cost_estimate=pl.CostEstimate(flops=2 * rows * depth * width * count, bytes_accessed=0, transcendentals=0),
    )(pos, *[a for h in hs for a in h], *ws, *heads, *after)


def retrace_kernel(length, q0, q1, rewards, actions, done_flags, behaviour, out):
    q = q0[...] + q1[...]
    count, steps = q.shape
    scaled = 4.0 * q
    weights = jnp.exp(scaled - jnp.max(scaled, axis=0, keepdims=True))
    probs = weights / jnp.sum(weights, axis=0, keepdims=True)
    value = jnp.sum(probs * q, axis=0, keepdims=True)
    hit = lax.broadcasted_iota(jnp.int32, (count, steps), 0) == actions[...]
    taken = jnp.sum(jnp.where(hit, q, 0.0), axis=0, keepdims=True)
    chosen = jnp.sum(jnp.where(hit, probs, 0.0), axis=0, keepdims=True)
    trace = 0.95 * jnp.minimum(1.0, chosen / behaviour[...])
    keep = 0.99 * (1.0 - done_flags[...].astype(jnp.float32))

    def later(x, by):
        return pltpu.roll(x, steps - by, axis=1)

    last = lax.broadcasted_iota(jnp.int32, (1, steps), 1) % length == length - 1
    factor = jnp.where(last, 0.0, keep * later(trace, 1))
    offset = jnp.where(last, taken, rewards[...] + keep * later(value - trace * taken, 1))
    by = 1
    while by < length:
        offset = offset + factor * later(offset, by)
        factor = factor * later(factor, by)
        by *= 2
    out[...] = offset


def retrace(q0, q1, rewards, actions, done_flags, behaviour, length):
    return pl.pallas_call(
        functools.partial(retrace_kernel, length),
        out_shape=jax.ShapeDtypeStruct(rewards.shape, jnp.float32),
        in_specs=[pl.BlockSpec(memory_space=pltpu.VMEM)] * 6,
        out_specs=pl.BlockSpec(memory_space=pltpu.VMEM),
    )(q0, q1, rewards, actions, done_flags, behaviour)


def per_device(dp, mp, observations, layer_weights, head_weights, rewards, actions, done_flags, behaviour):
    lines = dp // 2
    rank, group = lax.axis_index("mp"), lax.axis_index("dp")
    y = rank // 2
    cycle = list(range(0, dp, 2)) + list(range(dp - 1, 0, -2))
    at = jnp.where(group % 2 == 0, group // 2, dp - 1 - group // 2)

    def over(axis, pairs):
        return lambda a: lax.ppermute(a, axis, pairs)

    to_core = over("mp", [(i, i ^ 1) for i in range(mp)])
    to_y = over("mp", [(i, i ^ 2) for i in range(mp)])
    to_next = over("dp", [(cycle[i], cycle[(i + 1) % dp]) for i in range(dp)])
    to_last = over("dp", [(cycle[(i + 1) % dp], cycle[i]) for i in range(dp)])

    def came_from(step):
        spot = (at - step) % dp
        return jnp.where(spot < lines, 2 * spot, 2 * (dp - 1 - spot) + 1)

    rows = observations.shape[0] // 2
    seqs = rewards.shape[0] // 2
    flat = [lax.dynamic_slice_in_dim(a, y * seqs, seqs).reshape(1, -1) for a in (rewards, actions, done_flags, behaviour)]
    head = head_weights.T
    head_y = to_y(head)

    short, long = dp - 1 - lines, lines
    order = [rank, rank ^ 1, rank ^ 2, rank ^ 3]

    def run(columns, hs, **rest):
        ws, steps = [], []
        for col, (local, chains) in enumerate(columns):
            ws += [(a, j, col) for a, j in ((local, 0), *chains[0], *chains[1])]
            steps += [0, *range(1, len(chains[0]) + 1), *range(-1, -len(chains[1]) - 1, -1)]
        return layer(jnp.stack([came_from(step) for step in steps] + order), hs, ws, **rest)

    kept, sent = cut(observations, [y * rows, (1 - y) * rows], [rows, rows])
    w1, w2 = cut(layer_weights, [0, 1], [1, 1])
    w1_y = to_y(w1)
    kept_c = to_core(kept)
    turns = (long, short)
    ways = ([to_next(layer_weights)], [to_last(layer_weights)])
    sizes = [size for _, size in tiles_of(rows, TILE)]
    over_y = []
    parts, start, came, came_c = list(sizes), 0, [], []
    now = [*(way[0] for way in ways), w1_y, head_y]
    for i in range(1, dp - 1):
        if i == 1:
            (w2_gated,) = gate([[(w2, 0, 1)]], now)
            w2_y = to_y(w2_gated)
        build = []
        for way, turn in zip(ways, turns):
            last = way[-1]
            if i == 1:
                build.append([(last, 0, 1), (w1_y, 0, 1)])
            elif i == turn:
                build.append([(last, 1, 1), (way[0], 1, 1)])
            elif i == turn + 1:
                build.append([(last, 1, 1), (w2_y, 0, 1)])
            elif i == dp - 2:
                build.append([(over_y[0], len(build), 1)])
            else:
                build.append(None)
        if i == dp - 3:
            build.append([(way[-1], 1 if dp - 1 - turn == 3 else 0, 1) for way, turn in zip(ways, turns)])
        built = iter(gate([m for m in build if m], now)) if any(build) else None
        messages = [next(built) if m else way[-1] for m, way in zip(build, ways)]
        if i == dp - 3:
            over_y = [to_y(next(built))]
        if parts:
            size = parts.pop(0)
            (part,) = gate([[(sent, start, size)]], [*now, *messages, *(came[-1:] or [w2_y, *flat])])
            start += size
        for send, way, message in zip((to_next, to_last), ways, messages):
            way.append(send(message))
        if start and len(came) < len(sizes):
            came.append(to_y(part))
            came_c.append(to_core(came[-1]))
        now = [way[-1] for way in ways]
        if i == long + 1:
            first = [[], []]
            for way, turn in zip(ways, turns):
                first[0].append([(way[h - 1], 0) for h in range(1, turn + 1)])
                first[1].append([(way[h], 1 if h < turn else 0) for h in range(1, turn + 1)])
            h1 = run([(w1, first[0]), (w1_y, first[1])], [[kept], [kept_c], came, came_c], after=flat)
            mine, theirs = hold(h1, now + over_y)
            now = [*now, mine]
            h1 = [[mine], [to_core(mine)], [theirs], [to_core(theirs)]]
    second = [[], []]
    for n, (way, turn) in enumerate(zip(ways, turns)):
        second[0].append([(way[0], 1), (way[turn], 1)] + [(way[h], 0) for h in range(turn + 1, dp - 2)])
        second[1].append([(way[h], 1) for h in range(turn + 1, dp - 2)] + [(over_y[0], n), (way[-1], 0)])
    q = run([(w2, second[0]), (w2_y, second[1])], h1, heads=[head, head_y])
    own = retrace(q, to_core(q), *flat, rewards.shape[1])
    other = to_y(own)
    whole = jnp.concatenate([jnp.where(y == 0, own, other), jnp.where(y == 0, other, own)], axis=1)
    return whole.reshape(rewards.shape)


def solution(mesh):
    in_specs = (
        P("dp", "mp"),
        P(None, "dp", "mp"),
        P("mp", None),
        P("dp", None),
        P("dp", None),
        P("dp", None),
        P("dp", None),
    )
    out_specs = P("dp", None)
    return jax.shard_map(
        functools.partial(per_device, mesh.shape["dp"], mesh.shape["mp"]),
        mesh=mesh,
        in_specs=in_specs,
        out_specs=out_specs,
        check_vma=False,
    )
```

```python
import functools

import jax
import jax.numpy as jnp
from jax import lax
from jax.experimental import pallas as pl
from jax.experimental.pallas import tpu as pltpu
from jax.sharding import PartitionSpec as P

LANES = 128
TILE = 416


def tiles_of(rows, target):
    unit = LANES if rows % LANES == 0 else rows
    units = rows // unit
    count = max(1, -(-units * unit // target))
    sizes = [units // count + (1 if i < units % count else 0) for i in range(count)]
    starts = [sum(sizes[:i]) for i in range(count)]
    return [(s * unit, n * unit) for s, n in zip(starts, sizes) if n]


FREE = pl.CostEstimate(flops=0, bytes_accessed=0, transcendentals=0)


def cut_kernel(count, at, source, *refs):
    outs, sems = refs[-1 - count : -1], refs[-1]
    copies = []
    for i, out in enumerate(outs):
        first = at[i] if source.ndim > 2 else pl.multiple_of(at[i], 16)
        copies.append(pltpu.make_async_copy(source.at[pl.ds(first, out.shape[0])], out, sems.at[i]))
        copies[-1].start()
    for copy in copies:
        copy.wait()


def cut(source, at, sizes):
    return pl.pallas_call(
        functools.partial(cut_kernel, len(sizes)),
        out_shape=[jax.ShapeDtypeStruct((size, *source.shape[1:]), source.dtype) for size in sizes],
        in_specs=[pl.BlockSpec(memory_space=pltpu.SMEM), pl.BlockSpec(memory_space=pl.ANY)],
        out_specs=[pl.BlockSpec(memory_space=pltpu.VMEM)] * len(sizes),
        scratch_shapes=[pltpu.SemaphoreType.DMA((len(sizes),))],
        compiler_params=pltpu.CompilerParams(vmem_limit_bytes=40 * 1024 * 1024),
        cost_estimate=FREE,
    )(jnp.stack([jnp.asarray(a, jnp.int32) for a in at]), source)


def gate_kernel(messages, pieces, *refs):
    outs, sems = refs[-1 - len(messages) : -1], refs[-1]
    copies = []
    for out, message in zip(outs, messages):
        to = 0
        for operand, start, count in message:
            copies.append(
                pltpu.make_async_copy(refs[operand].at[pl.ds(start, count)], out.at[pl.ds(to, count)], sems.at[len(copies)])
            )
            copies[-1].start()
            to += count
    for copy in copies:
        copy.wait()


def gate(messages, after=()):
    arrays, plan, shapes = [], [], []
    for message in messages:
        plan.append([])
        for array, start, count in message:
            if not any(array is other for other in arrays):
                arrays.append(array)
            plan[-1].append(([array is other for other in arrays].index(True), start, count))
        first = message[0][0]
        shapes.append(jax.ShapeDtypeStruct((sum(n for _, _, n in message), *first.shape[1:]), first.dtype))
    pieces = sum(len(message) for message in messages)
    held = sum(shape.size * shape.dtype.itemsize for shape in shapes)
    return pl.pallas_call(
        functools.partial(gate_kernel, plan, pieces),
        out_shape=shapes,
        in_specs=[pl.BlockSpec(memory_space=pl.ANY)] * (len(arrays) + len(after)),
        out_specs=[pl.BlockSpec(memory_space=pltpu.VMEM)] * len(shapes),
        scratch_shapes=[pltpu.SemaphoreType.DMA((pieces,))],
        compiler_params=pltpu.CompilerParams(vmem_limit_bytes=held + 1024 * 1024),
        cost_estimate=FREE,
    )(*arrays, *after)


def hold_kernel(*refs):
    pass


def hold(arrays, after):
    anywhere = pl.BlockSpec(memory_space=pl.ANY)
    return pl.pallas_call(
        hold_kernel,
        out_shape=[jax.ShapeDtypeStruct(a.shape, a.dtype) for a in arrays],
        in_specs=[anywhere] * (len(arrays) + len(after)),
        out_specs=[anywhere] * len(arrays),
        input_output_aliases={i: i for i in range(len(arrays))},
        compiler_params=pltpu.CompilerParams(vmem_limit_bytes=1024 * 1024),
        cost_estimate=FREE,
    )(*arrays, *after)


def layer_kernel(kinds, blocks, tiles, width, headed, waited, *refs):
    refs = list(refs)
    pos = refs.pop(0)
    hs = [[refs.pop(0) for _ in range(kind)] for kind in kinds]
    ws = [refs.pop(0) for _ in blocks]
    heads = [refs.pop(0) for _ in range(headed)]
    del refs[:waited]
    hv, wv = refs[-6:-4] if not headed else refs[-4:-2]
    count = wv.shape[1] // width
    outs = [refs.pop(0) for _ in range(1 if headed else count)]
    refs = refs[2:]
    ov = None if headed else refs.pop(0)
    hsem, wsem = refs.pop(0), refs.pop(0)
    osem = None if headed else refs.pop(0)

    w_copies = []
    for i, (w, (j, col)) in enumerate(zip(ws, blocks)):
        height = w.shape[1]
        to = wv.at[pl.ds(pl.multiple_of(pos[i] * height, height), height), pl.ds(col * width, width)]
        w_copies.append(pltpu.make_async_copy(w.at[j], to, wsem.at[i]))
    h_copies = []
    for t, (start, size) in enumerate(tiles):
        h_copies.append([])
        for i, h in enumerate(hs):
            wide = h[0].shape[1]
            to = hv.at[pl.ds(start, size), pl.ds(pl.multiple_of(pos[len(blocks) + i] * wide, wide), wide)]
            source = h[t] if len(h) > 1 else h[0].at[pl.ds(start, size)]
            h_copies[-1].append(pltpu.make_async_copy(source, to, hsem.at[t, i]))
    w_columns = [[copy for copy, (_, at) in zip(w_copies, blocks) if at == col] for col in range(count)]
    for copy in h_copies[0] + w_columns[0]:
        copy.start()
    out_copies = []
    for t, (start, size) in enumerate(tiles):
        rows = pl.ds(start, size)
        for copy in h_copies[t]:
            copy.wait()
        total = None
        for col in range(count):
            if t == 0:
                for copy in w_columns[col]:
                    copy.wait()
                for copy in w_columns[col + 1] if col + 1 < count else []:
                    copy.start()
            if col == 0 and t + 1 < len(tiles):
                for copy in h_copies[t + 1]:
                    copy.start()
            units = pl.ds(col * width, width)
            summed = jnp.dot(hv[rows, :], wv[:, units], preferred_element_type=jnp.float32)
            hidden = jnp.maximum(summed, 0.0).astype(jnp.bfloat16)
            if headed:
                q = lax.dot_general(
                    heads[col][...], hidden, (((1,), (1,)), ((), ())), preferred_element_type=jnp.float32
                )
                total = q if total is None else total + q
            else:
                ov[rows, units] = hidden
                out_copies.append(pltpu.make_async_copy(ov.at[rows, units], outs[col].at[rows], osem.at[t, col]))
                out_copies[-1].start()
        if headed:
            outs[0][:, rows] = total
    for copy in out_copies:
        copy.wait()


def layer(pos, hs, ws, heads=(), after=()):
    rows = hs[0][0].shape[0]
    tiles = tiles_of(rows, TILE)
    blocks = [(j, col) for _, j, col in ws]
    ws = [w for w, _, _ in ws]
    count = 1 + max(col for _, col in blocks)
    width = ws[0].shape[2]
    depth = ws[0].shape[1] * len(ws) // count
    headed = len(heads)
    vmem = pl.BlockSpec(memory_space=pltpu.VMEM)
    anywhere = pl.BlockSpec(memory_space=pl.ANY)
    scratch = [pltpu.VMEM((rows, depth), jnp.bfloat16), pltpu.VMEM((depth, width * count), jnp.bfloat16)]
    if not headed:
        scratch.append(pltpu.VMEM((rows, width * count), jnp.bfloat16))
    scratch += [pltpu.SemaphoreType.DMA((len(tiles), len(hs))), pltpu.SemaphoreType.DMA((len(ws),))]
    if headed:
        out_shape = jax.ShapeDtypeStruct((heads[0].shape[0], rows), jnp.float32)
    else:
        scratch.append(pltpu.SemaphoreType.DMA((len(tiles), count)))
        out_shape = [jax.ShapeDtypeStruct((rows, width), jnp.bfloat16)] * count
    return pl.pallas_call(
        functools.partial(layer_kernel, [len(h) for h in hs], blocks, tiles, width, headed, len(after)),
        out_shape=out_shape,
        in_specs=[pl.BlockSpec(memory_space=pltpu.SMEM)]
        + [anywhere] * (sum(len(h) for h in hs) + len(ws))
        + [vmem] * headed
        + [anywhere] * len(after),
        out_specs=vmem if headed else [anywhere] * count,
        scratch_shapes=scratch,
        compiler_params=pltpu.CompilerParams(vmem_limit_bytes=52 * 1024 * 1024),
        cost_estimate=pl.CostEstimate(flops=2 * rows * depth * width * count, bytes_accessed=0, transcendentals=0),
    )(pos, *[a for h in hs for a in h], *ws, *heads, *after)


def retrace_kernel(length, q0, q1, rewards, actions, done_flags, behaviour, out):
    q = q0[...] + q1[...]
    count, steps = q.shape
    scaled = 4.0 * q
    weights = jnp.exp(scaled - jnp.max(scaled, axis=0, keepdims=True))
    share = 1.0 / jnp.sum(weights, axis=0, keepdims=True)
    value = jnp.sum(weights * q, axis=0, keepdims=True) * share
    hit = lax.broadcasted_iota(jnp.int32, (count, steps), 0) == actions[...]
    taken = jnp.sum(jnp.where(hit, q, 0.0), axis=0, keepdims=True)
    chosen = jnp.sum(jnp.where(hit, weights, 0.0), axis=0, keepdims=True) * share
    trace = 0.95 * jnp.minimum(1.0, chosen / behaviour[...])
    keep = 0.99 * (1.0 - done_flags[...].astype(jnp.float32))

    def later(x, by):
        return pltpu.roll(x, steps - by, axis=1)

    last = lax.broadcasted_iota(jnp.int32, (1, steps), 1) % length == length - 1
    factor = jnp.where(last, 0.0, keep * later(trace, 1))
    offset = jnp.where(last, taken, rewards[...] + keep * later(value - trace * taken, 1))
    by = 1
    while by < length:
        offset = offset + factor * later(offset, by)
        factor = factor * later(factor, by)
        by *= 2
    out[...] = offset


def retrace(q0, q1, rewards, actions, done_flags, behaviour, length):
    return pl.pallas_call(
        functools.partial(retrace_kernel, length),
        out_shape=jax.ShapeDtypeStruct(rewards.shape, jnp.float32),
        in_specs=[pl.BlockSpec(memory_space=pltpu.VMEM)] * 6,
        out_specs=pl.BlockSpec(memory_space=pltpu.VMEM),
    )(q0, q1, rewards, actions, done_flags, behaviour)


def per_device(dp, mp, observations, layer_weights, head_weights, rewards, actions, done_flags, behaviour):
    lines = dp // 2
    rank, group = lax.axis_index("mp"), lax.axis_index("dp")
    y = rank // 2
    cycle = list(range(0, dp, 2)) + list(range(dp - 1, 0, -2))
    at = jnp.where(group % 2 == 0, group // 2, dp - 1 - group // 2)

    def over(axis, pairs):
        return lambda a: lax.ppermute(a, axis, pairs)

    to_core = over("mp", [(i, i ^ 1) for i in range(mp)])
    to_y = over("mp", [(i, i ^ 2) for i in range(mp)])
    to_next = over("dp", [(cycle[i], cycle[(i + 1) % dp]) for i in range(dp)])
    to_last = over("dp", [(cycle[(i + 1) % dp], cycle[i]) for i in range(dp)])

    def came_from(step):
        spot = (at - step) % dp
        return jnp.where(spot < lines, 2 * spot, 2 * (dp - 1 - spot) + 1)

    rows = observations.shape[0] // 2
    seqs = rewards.shape[0] // 2
    flat = [lax.dynamic_slice_in_dim(a, y * seqs, seqs).reshape(1, -1) for a in (rewards, actions, done_flags, behaviour)]
    head = head_weights.T
    head_y = to_y(head)

    short, long = dp - 1 - lines, lines
    order = [rank, rank ^ 1, rank ^ 2, rank ^ 3]

    def run(columns, hs, **rest):
        ws, steps = [], []
        for col, (local, chains) in enumerate(columns):
            ws += [(a, j, col) for a, j in ((local, 0), *chains[0], *chains[1])]
            steps += [0, *range(1, len(chains[0]) + 1), *range(-1, -len(chains[1]) - 1, -1)]
        return layer(jnp.stack([came_from(step) for step in steps] + order), hs, ws, **rest)

    kept, sent = cut(observations, [y * rows, (1 - y) * rows], [rows, rows])
    w1, w2 = cut(layer_weights, [0, 1], [1, 1])
    w1_y = to_y(w1)
    kept_c = to_core(kept)
    turns = (long, short)
    ways = ([to_next(layer_weights)], [to_last(layer_weights)])
    sizes = [size for _, size in tiles_of(rows, TILE)]
    over_y = []
    parts, start, came, came_c = list(sizes), 0, [], []
    now = [*(way[0] for way in ways), w1_y, head_y]
    for i in range(1, dp - 1):
        if i == 1:
            (w2_gated,) = gate([[(w2, 0, 1)]], now)
            w2_y = to_y(w2_gated)
        build = []
        for way, turn in zip(ways, turns):
            last = way[-1]
            if i == 1:
                build.append([(last, 0, 1), (w1_y, 0, 1)])
            elif i == turn:
                build.append([(last, 1, 1), (way[0], 1, 1)])
            elif i == turn + 1:
                build.append([(last, 1, 1), (w2_y, 0, 1)])
            elif i == dp - 2:
                build.append([(over_y[0], len(build), 1)])
            else:
                build.append(None)
        if i == dp - 3:
            build.append([(way[-1], 1 if dp - 1 - turn == 3 else 0, 1) for way, turn in zip(ways, turns)])
        built = iter(gate([m for m in build if m], now)) if any(build) else None
        messages = [next(built) if m else way[-1] for m, way in zip(build, ways)]
        if i == dp - 3:
            over_y = [to_y(next(built))]
        if parts:
            size = parts.pop(0)
            (part,) = gate([[(sent, start, size)]], [*now, *messages, *(came[-1:] or [w2_y, *flat])])
            start += size
        for send, way, message in zip((to_next, to_last), ways, messages):
            way.append(send(message))
        if start and len(came) < len(sizes):
            came.append(to_y(part))
            came_c.append(to_core(came[-1]))
        now = [way[-1] for way in ways]
        if i == long + 1:
            first = [[], []]
            for way, turn in zip(ways, turns):
                first[0].append([(way[h - 1], 0) for h in range(1, turn + 1)])
                first[1].append([(way[h], 1 if h < turn else 0) for h in range(1, turn + 1)])
            h1 = run([(w1, first[0]), (w1_y, first[1])], [[kept], [kept_c], came, came_c], after=flat)
            mine, theirs = hold(h1, now + over_y)
            now = [*now, mine]
            h1 = [[mine], [to_core(mine)], [theirs], [to_core(theirs)]]
    second = [[], []]
    for n, (way, turn) in enumerate(zip(ways, turns)):
        second[0].append([(way[0], 1), (way[turn], 1)] + [(way[h], 0) for h in range(turn + 1, dp - 2)])
        second[1].append([(way[h], 1) for h in range(turn + 1, dp - 2)] + [(over_y[0], n), (way[-1], 0)])
    q = run([(w2, second[0]), (w2_y, second[1])], h1, heads=[head, head_y])
    own = retrace(q, to_core(q), *flat, rewards.shape[1])
    other = to_y(own)
    whole = jnp.concatenate([jnp.where(y == 0, own, other), jnp.where(y == 0, other, own)], axis=1)
    return whole.reshape(rewards.shape)


def solution(mesh):
    in_specs = (
        P("dp", "mp"),
        P(None, "dp", "mp"),
        P("mp", None),
        P("dp", None),
        P("dp", None),
        P("dp", None),
        P("dp", None),
    )
    out_specs = P("dp", None)
    return jax.shard_map(
        functools.partial(per_device, mesh.shape["dp"], mesh.shape["mp"]),
        mesh=mesh,
        in_specs=in_specs,
        out_specs=out_specs,
        check_vma=False,
    )
```
